32 devices in a mesh: ctx: 8 (over z, y), tp: 2 (over x), probe: 2 (over core).
Axes of the slice: x: 2, y: 2, z: 4, core: 2. Of those that a mesh axis runs over, the one named last changes fastest.
Arguments:
- latent: float32 [1024, 3072], P('ctx', 'tp'), may hold values from -6 to 6
- probes: int32 [2, 1024, 3072], P('probe', 'ctx', 'tp'), may hold values from 0 to 1
- modulation: float32 [2, 3, 3072], replicated, may hold values from -3 to 3
- pattern: int32 [8, 8], P('ctx'), may hold values from 0 to 7, as said below
- w_qkv: bfloat16 [3072, 3, 3072], P(None, None, 'tp'), may hold values from -0.109375 to 0.109375
- w_out: bfloat16 [3072, 3072], P('tp'), may hold values from -0.109375 to 0.109375
- w_up: bfloat16 [3072, 6144], P('ctx', 'tp'), may hold values from -0.109375 to 0.109375
- w_down: bfloat16 [6144, 3072], P('tp', 'ctx'), may hold values from -0.078125 to 0.078125
- q_gain: float32 [3072], P('tp'), may hold values from 0.5 to 5.1, as said below
- k_gain: float32 [3072], P('tp'), may hold values from 0.5 to 2
Outputs:
- latent_out: float32 [1024, 3072], P('ctx', 'tp')
- density_change: float32 [1024], P('ctx')
The draws below stay inside these ranges and needn't reach their ends.
Inputs may be any that keep to these rules, and one draw needn't show every extreme that they name: `pattern`: row q lists key blocks for query block q: its first entry is q; the next entries are distinct blocks other than q up to a count of 1 to 8, after which every entry is q again; row 0 lists 8 distinct blocks. `q_gain`: positive gains.
All inputs are finite; a program needn't handle non-finite values.
Results may differ from the reference program's by a relative error of at most 0.034.
Values may be sent and summed in bfloat16 or wider, within the bound.
No kernel may reach another device: no remote copies, remote signals or barrier semaphores. Data moves between devices by JAX's collectives and lax.ppermute only.
A program may use at most 192 MiB of HBM per device.

```python
import math
import jax
import jax.numpy as jnp
from jax import lax

D = 3072
H = 24
HD = 128
FF = 6144
BLK = 128
K_SEL = 8
STEPS = 2
TOKENS = 1024
NB = 8
PROBES = 2
N_TP = 2


def draw_pattern(key, part):
    blocks = jnp.arange(NB, dtype=jnp.int32)
    row_keys = jax.random.split(jax.random.fold_in(key, 11), NB)
    offsets = jax.vmap(lambda row_key: jax.random.permutation(row_key, NB - 1)[:K_SEL - 1])(row_keys) + 1
    counts = jax.random.randint(jax.random.fold_in(key, 12), (NB,), 1, K_SEL + 1)
    counts = counts.at[0].set(K_SEL)
    others = (blocks[:, None] + offsets.astype(jnp.int32)) % NB
    columns = jnp.arange(1, K_SEL, dtype=jnp.int32)
    others = jnp.where(columns[None, :] < counts[:, None], others, blocks[:, None])
    return jnp.concatenate([blocks[:, None], others], axis=1).astype(jnp.int32)


def draw_q_gain(key, part):
    head_level = jax.random.uniform(jax.random.fold_in(key, 21), (H, 1), jnp.float32)
    fine_level = jax.random.uniform(jax.random.fold_in(key, 22), (H, HD), jnp.float32, 0.8, 1.25)
    head_scale = jnp.exp((head_level - 0.5) * math.log(2.0))
    return (head_scale * fine_level).reshape(H * HD).astype(jnp.float32)


def plant(array, stream_key, low, high):
    dims = array.shape
    index_at = [jax.random.randint(jax.random.fold_in(stream_key, axis), (), 0, dims[axis]) for axis in range(len(dims))]
    array = array.at[tuple(index_at)].set(low)
    longest = dims.index(max(dims))
    index_at[longest] = (index_at[longest] + 1) % dims[longest]
    return array.at[tuple(index_at)].set(high)


def levels(own_key, extent, cuts, least, high):
    loudness = 1.0
    for position, blocks in cuts:
        heights = jax.random.uniform(jax.random.fold_in(jax.random.fold_in(own_key, 6), position), (blocks,), jnp.float32, least / len(cuts), high / len(cuts))
        loudness = loudness * jnp.repeat(jnp.exp(heights), extent[position] // blocks).reshape((-1,) + (1,) * (len(extent) - 1 - position))
    return loudness


def gaussian(stream_key, extent, scale, bound, pieces=(), kind=jnp.bfloat16):
    entries = scale * jax.random.normal(stream_key, extent, jnp.float32)
    if pieces:
        entries = entries * levels(stream_key, extent, pieces, -0.22, 0.18)
    return jnp.clip(entries, -bound, bound).astype(kind)


def setup_inputs(seed: int = 0) -> dict:
    keys = jax.random.split(jax.random.key(seed), 11)
    return {
        "latent": gaussian(keys[0], (TOKENS, D), 1.0, 6.0, ((0, 8), (1, 2)), jnp.float32),
        "probes": plant(jax.random.randint(keys[1], (PROBES, TOKENS, D), 0, 2), jax.random.fold_in(keys[1], 1), 0, 1).astype(jnp.int32),
        "modulation": gaussian(keys[2], (STEPS, 3, D), 0.5, 3.0, (), jnp.float32),
        "pattern": draw_pattern(jax.random.fold_in(keys[10], 71), 0),
        "w_qkv": gaussian(keys[4], (D, 3, H * HD), D ** -0.5, 0.109375, ((2, 2),)),
        "w_out": gaussian(keys[5], (H * HD, D), (H * HD) ** -0.5, 0.109375, ((0, 2),)),
        "w_up": gaussian(keys[6], (D, FF), D ** -0.5, 0.109375, ((0, 8), (1, 2))),
        "w_down": gaussian(keys[7], (FF, D), FF ** -0.5, 0.078125, ((0, 2), (1, 8))),
        "q_gain": draw_q_gain(jax.random.fold_in(keys[10], 71), 0),
        "k_gain": jnp.clip(jnp.exp(math.log(2.0) - 1.3862944 * jax.random.uniform(keys[9], (H * HD,), jnp.float32) ** levels(keys[9], (H * HD,), ((0, 2),), -0.2, 0.2)), 0.5, 2.0),
    }


EPS = 1e-06

def rounded(values):
    return lax.optimization_barrier(values.astype(jnp.bfloat16)).astype(jnp.float32)

def layer_norm(rows):
    row_mean = lax.optimization_barrier(jnp.mean(rows, axis=-1, keepdims=True))
    row_var = lax.optimization_barrier(jnp.mean(rows * rows, axis=-1, keepdims=True)) - row_mean * row_mean
    return (rows - row_mean) * lax.rsqrt(row_var + EPS)

def head_norm(projected, head_gain):
    head_view = projected.reshape(projected.shape[0], H, HD)
    inv_std = lax.rsqrt(lax.optimization_barrier(jnp.mean(head_view * head_view, axis=-1, keepdims=True)) + EPS)
    return (head_view * inv_std * head_gain.reshape(H, HD)).astype(jnp.bfloat16)

def block_mask(pattern):
    blocks = jnp.arange(NB, dtype=jnp.int32)
    listed = jnp.any(pattern[:, :, None] == blocks[None, None, :], axis=1)
    return jnp.repeat(jnp.repeat(listed, BLK, axis=0), BLK, axis=1)

def velocity(latent, mod_row, allowed, w_qkv, w_out, w_up, w_down, q_gain, k_gain):
    normed = (layer_norm(latent) * (1.0 + mod_row[1]) + mod_row[0]).astype(jnp.bfloat16)
    q_proj = jnp.dot(normed, w_qkv[:, 0], preferred_element_type=jnp.float32)
    k_proj = jnp.dot(normed, w_qkv[:, 1], preferred_element_type=jnp.float32)
    v_proj = jnp.dot(normed, w_qkv[:, 2], preferred_element_type=jnp.float32)
    q_rows = head_norm(q_proj, q_gain)
    k_rows = head_norm(k_proj, k_gain)
    v_rows = v_proj.astype(jnp.bfloat16).reshape(TOKENS, H, HD)

    def one_head(items):
        query_rows, key_rows, value_rows = items
        scores = jnp.dot(query_rows, key_rows.T, preferred_element_type=jnp.float32) / math.sqrt(HD)
        scores = jnp.where(allowed, scores, -1e+30)
        weights = jax.nn.softmax(scores, axis=-1)
        return jnp.dot(weights, value_rows.astype(jnp.float32), precision=lax.Precision.HIGHEST)
    outputs = lax.map(one_head, (q_rows.transpose(1, 0, 2), k_rows.transpose(1, 0, 2), v_rows.transpose(1, 0, 2)))
    attended = outputs.transpose(1, 0, 2).reshape(TOKENS, H * HD).astype(jnp.bfloat16)
    hidden = jax.nn.gelu(jnp.dot(normed, w_up, preferred_element_type=jnp.float32), approximate=True).astype(jnp.bfloat16)
    head_cols = H * HD // N_TP
    hidden_cols = FF // N_TP
    branch_sum = jnp.zeros((TOKENS, D), jnp.float32)
    for group in range(N_TP):
        group_part = jnp.dot(attended[:, group * head_cols:(group + 1) * head_cols], w_out[group * head_cols:(group + 1) * head_cols], preferred_element_type=jnp.float32)
        group_part = group_part + jnp.dot(hidden[:, group * hidden_cols:(group + 1) * hidden_cols], w_down[group * hidden_cols:(group + 1) * hidden_cols], preferred_element_type=jnp.float32)
        branch_sum = branch_sum + rounded(group_part)
    return mod_row[2] * branch_sum

def reference(latent, probes, modulation, pattern, w_qkv, w_out, w_up, w_down, q_gain, k_gain):
    allowed = block_mask(pattern)
    probe_signs = 2.0 * probes.astype(jnp.float32) - 1.0
    change = jnp.zeros((TOKENS,), jnp.float32)
    step_size = 1.0 / STEPS
    for euler_step in range(STEPS):
        mod_row = modulation[euler_step]

        def field_map(rows):
            return velocity(rows, mod_row, allowed, w_qkv, w_out, w_up, w_down, q_gain, k_gain)
        for probe_idx in range(PROBES):
            speed, tangent = jax.jvp(field_map, (latent,), (probe_signs[probe_idx],))
            change = change + lax.optimization_barrier(jnp.sum(probe_signs[probe_idx] * tangent, axis=1))
        latent = latent + step_size * speed
    density_change = -step_size * change / (PROBES * math.sqrt(D))
    return (latent, density_change)
```

```python
import math

import jax
import jax.numpy as jnp
from jax import lax
from jax.sharding import PartitionSpec as P

HD = 128
BLK = 128
STEPS = 2
EPS = 1e-06
NEG_BIG = -1e30
F32 = jnp.float32
BF16 = jnp.bfloat16


def dot(a, b):
    return jnp.dot(a, b, preferred_element_type=F32)


def dot_t(a, b):
    return lax.dot_general(a, b, (((1,), (1,)), ((), ())), preferred_element_type=F32)


def cycle_of(size):
    return list(range(0, size, 2)) + list(range(size - 1, 0, -2))


def ring_shift(x, cycle, shift):
    size = len(cycle)
    pairs = [(cycle[i], cycle[(i + shift) % size]) for i in range(size)]
    return lax.ppermute(x, "ctx", pairs)


def ring_gather(own, cycle, split_axis):
    size = len(cycle)
    reach = size // 2
    slots = [None] * size
    slots[0] = own
    fore = back = own
    for hop in range(1, reach):
        back = ring_shift(back, cycle, 1)
        fore = ring_shift(fore, cycle, -1)
        slots[size - hop] = back
        slots[hop] = fore
    first, second = jnp.split(own, 2, axis=split_axis) if reach == 1 else (None, None)
    first = jnp.split(back, 2, axis=split_axis)[0]
    second = jnp.split(fore, 2, axis=split_axis)[1]
    first = ring_shift(first, cycle, 1)
    second = ring_shift(second, cycle, -1)
    slots[reach] = jnp.concatenate([first, second], axis=split_axis)
    return slots


def ring_reduce(parts, cycle, wire):
    size = len(cycle)
    reach = size // 2
    width = parts[0].shape[1] // 2
    far = parts[reach].astype(wire)
    up = ring_shift(far[:, :width], cycle, 1).astype(F32)
    down = ring_shift(far[:, width:], cycle, -1).astype(F32)
    for hop in range(reach - 1, 0, -1):
        up_part, down_part = parts[hop], parts[size - hop]
        if hop == reach - 1:
            up = jnp.concatenate([up_part[:, :width] + up, up_part[:, width:].astype(F32)], axis=1)
            down = jnp.concatenate([down_part[:, :width].astype(F32), down_part[:, width:] + down], axis=1)
        else:
            up = up_part + up
            down = down_part + down
        up = ring_shift(up.astype(wire), cycle, 1).astype(F32)
        down = ring_shift(down.astype(wire), cycle, -1).astype(F32)
    return parts[0] + up + down


def swap(x, axis):
    return lax.ppermute(x, axis, [(0, 1), (1, 0)])


def join_tp(own, axis):
    if lax.axis_size("tp") == 2:
        other = swap(own, "tp")
        first = lax.axis_index("tp") == 0
        low = jnp.where(first, own, other)
        high = jnp.where(first, other, own)
        return jnp.concatenate([low, high], axis=axis)
    return lax.all_gather(own, "tp", axis=axis, tiled=True)


def sum_tp(own):
    if lax.axis_size("tp") == 2:
        return own.astype(F32) + swap(own, "tp").astype(F32)
    return jnp.sum(lax.all_gather(own, "tp", axis=0, tiled=False).astype(F32), axis=0)


def join_probe(own, axis):
    other = swap(own, "probe")
    first = lax.axis_index("probe") == 0
    return jnp.concatenate([jnp.where(first, own, other), jnp.where(first, other, own)], axis=axis)


def exchange(pieces, cycle):
    size = len(cycle)
    got = [None] * size
    got[0] = pieces[0]
    for shift in sorted(range(1, size), key=lambda s: -min(s, size - s)):
        got[(size - shift) % size] = ring_shift(pieces[shift], cycle, shift)
    return got


def head_parts(raw, index):
    return raw[:, index * HD:(index + 1) * HD]


def head_norm(raw, gain):
    inv = lax.rsqrt(jnp.mean(raw * raw, axis=1, keepdims=True) + EPS)
    return (raw * inv * gain).astype(BF16), inv


def head_norm_tangent(raw, tan, inv, gain):
    tan_inv = -inv * inv * inv * jnp.mean(raw * tan, axis=1, keepdims=True)
    return ((tan * inv + raw * tan_inv) * gain).astype(BF16)


def local(latent, probes, modulation, pattern, w_qkv, w_out, w_up, w_down, q_gain, k_gain):
    ctx_size = lax.axis_size("ctx")
    tp_size = lax.axis_size("tp")
    cycle = cycle_of(ctx_size)
    row_count, local_width = latent.shape
    half = row_count // 2
    full_width = local_width * tp_size
    tokens = row_count * ctx_size
    heads_local = q_gain.shape[0] // HD
    groups = math.gcd(heads_local, ctx_size)
    heads_own = heads_local // groups
    head_width = heads_own * HD
    query_rows = groups * row_count
    unit_total = w_up.shape[1]
    units = unit_total // ctx_size
    step_size = 1.0 / STEPS
    score_scale = 1.0 / math.sqrt(HD)

    ctx_index = lax.axis_index("ctx")
    probe_index = lax.axis_index("probe")
    tp_index = lax.axis_index("tp")
    cycle_arr = jnp.array(cycle, jnp.int32)
    place = jnp.array([cycle.index(i) for i in range(ctx_size)], jnp.int32)
    ring_index = place[ctx_index]
    slot_owner = cycle_arr[(ring_index + jnp.arange(ctx_size)) % ctx_size]
    owner_slot = (place - ring_index) % ctx_size
    group = ring_index % groups

    lat_half = lax.dynamic_slice_in_dim(latent, probe_index * half, half, 0)
    rows = join_tp(lat_half, 1)

    up_half = lax.dynamic_slice_in_dim(w_up, probe_index * (w_up.shape[0] // 2), w_up.shape[0] // 2, 0)
    up_pieces = [
        lax.dynamic_slice_in_dim(up_half, slot_owner[k] * units, units, 1) for k in range(ctx_size)
    ]
    up_got = jnp.stack(exchange(up_pieces, cycle))[owner_slot]
    up_other = swap(up_got, "probe")
    first = probe_index == 0
    up_own = jnp.stack([jnp.where(first, up_got, up_other), jnp.where(first, up_other, up_got)], axis=1)
    up_own = up_own.reshape(full_width, units)

    down_pieces = [
        lax.dynamic_slice_in_dim(w_down, slot_owner[k] * units + probe_index * (units // 2), units // 2, 0)
        for k in range(ctx_size)
    ]
    down_got = jnp.stack(exchange(down_pieces, cycle))[owner_slot]
    down_got = down_got.transpose(1, 0, 2).reshape(units // 2, full_width)
    down_own = join_probe(down_got, 0)

    qkv_own = lax.dynamic_slice_in_dim(w_qkv, group * head_width, head_width, 2)
    q_weight, k_weight, v_weight = (qkv_own[:, part] for part in range(3))
    out_own = lax.dynamic_slice_in_dim(w_out, group * head_width, head_width, 0)
    q_gain_own = lax.dynamic_slice_in_dim(q_gain, group * head_width, head_width, 0)[None]
    k_gain_own = lax.dynamic_slice_in_dim(k_gain, group * head_width, head_width, 0)[None]

    signs_local = (2 * probes[0] - 1).astype(BF16)
    signs_local = signs_local.reshape(2, half, local_width)
    signs_local = jnp.where(first, signs_local, signs_local[::-1]).reshape(row_count, local_width)
    sign_slots = ring_gather(signs_local, cycle, 1)
    signs = join_tp(jnp.concatenate(sign_slots, axis=0), 1)
    own_signs = signs[:half].astype(F32)
    other_signs = swap(signs[half:row_count], "probe").astype(F32)
    own_mean = jnp.mean(own_signs, axis=1)
    other_mean = jnp.mean(other_signs, axis=1)

    lists = lax.all_gather(pattern, "ctx", axis=0, tiled=True)
    listed = jnp.any(lists[slot_owner[:groups]][:, :, None] == slot_owner[None, None, :], axis=1)
    allowed = jnp.repeat(jnp.repeat(listed, row_count, axis=0), row_count, axis=1)

    estimate = jnp.zeros((tokens,), F32)
    for step in range(STEPS):
        mod = modulation[step]
        shift, stretch, gate = mod[0][None], 1.0 + mod[1][None], mod[2][None]

        row_mean = jnp.mean(rows, axis=1, keepdims=True)
        row_var = jnp.mean(rows * rows, axis=1, keepdims=True) - row_mean * row_mean
        inv_std = lax.rsqrt(row_var + EPS)
        normed_own = ((rows - row_mean) * inv_std * stretch + shift).astype(BF16)
        slots = ring_gather(normed_own, cycle, 1)
        normed = jnp.concatenate(
            [piece for slot in slots for piece in (slot, swap(slot, "probe"))], axis=0
        )
        q_raw = dot(normed[:query_rows], q_weight)
        k_raw = dot(normed, k_weight)
        v_raw = dot(normed, v_weight)

        stretch_bf = stretch.astype(BF16)
        scaled = signs * stretch_bf
        gated = (signs.astype(F32) * gate).astype(BF16)
        q_sign = dot(scaled[:query_rows], q_weight)
        k_sign = dot(scaled, k_weight)
        v_sign = dot(scaled, v_weight)
        up_sign = dot(scaled, up_own)
        down_back = dot_t(gated, down_own)
        out_back = dot_t(gated[:query_rows], out_own)
        pair = jnp.concatenate([stretch_bf, shift.astype(BF16), jnp.zeros((14, full_width), BF16)], axis=0)
        q_pair, k_pair, v_pair, up_pair = (dot(pair, w) for w in (q_weight, k_weight, v_weight, up_own))

        flat_mean, flat_inv = row_mean[:, 0], inv_std[:, 0]
        scalars = [flat_inv]
        for sign_rows, sign_mean in ((own_signs, own_mean), (other_signs, other_mean)):
            tan_var = 2.0 * (jnp.mean(rows * sign_rows, axis=1) - flat_mean * sign_mean)
            scalars += [flat_inv * sign_mean, 0.5 * tan_var * flat_inv * flat_inv]
        own_scalars = jnp.stack(scalars[:3], axis=1)
        cross_scalars = jnp.stack([scalars[0]] + scalars[3:], axis=1)
        block_scalars = jnp.concatenate([own_scalars, swap(cross_scalars, "probe")], axis=0)
        gathered = lax.all_gather(block_scalars, "ctx", axis=0, tiled=False)
        gathered = gathered[slot_owner].reshape(tokens, 3)
        t_inv, t_mean, t_var = (gathered[:, i:i + 1] for i in range(3))

        def tangent(raw, sign, consts, count):
            return (
                t_inv[:count] * sign - t_mean[:count] * consts[0:1] - t_var[:count] * (raw - consts[1:2])
            )

        dq_raw = tangent(q_raw, q_sign, q_pair, query_rows)
        dk_raw = tangent(k_raw, k_sign, k_pair, tokens)
        dv_raw = tangent(v_raw, v_sign, v_pair, tokens)

        attended_heads = []
        attn_estimate = jnp.zeros((query_rows,), F32)
        for head in range(heads_own):
            q_head, k_head, v_head = (head_parts(raw, head) for raw in (q_raw, k_raw, v_raw))
            q_gain_head, k_gain_head = head_parts(q_gain_own, head), head_parts(k_gain_own, head)
            q_n, q_inv = head_norm(q_head, q_gain_head)
            k_n, k_inv = head_norm(k_head, k_gain_head)
            v_n = v_head.astype(BF16)
            scores = dot_t(q_n, k_n) * score_scale
            scores = jnp.where(allowed, scores, NEG_BIG)
            top = jnp.max(scores, axis=1, keepdims=True)
            weights = jnp.where(allowed, jnp.exp(scores - top), 0.0)
            inv_total = 1.0 / jnp.sum(weights, axis=1, keepdims=True)
            weights_bf = weights.astype(BF16)
            attended = dot(weights_bf, v_n) * inv_total
            attended_heads.append(attended.astype(BF16))

            dq_n = head_norm_tangent(q_head, head_parts(dq_raw, head), q_inv, q_gain_head)
            dk_n = head_norm_tangent(k_head, head_parts(dk_raw, head), k_inv, k_gain_head)
            dv_n = head_parts(dv_raw, head).astype(BF16)
            tan_scores = dot_t(
                jnp.concatenate([dq_n, q_n], axis=1), jnp.concatenate([k_n, dk_n], axis=1)
            ) * score_scale
            weighted = weights * tan_scores
            tan_sum = jnp.sum(weighted, axis=1, keepdims=True) * inv_total
            tan_out = (dot(weights_bf, dv_n) + dot(weighted.astype(BF16), v_n)) * inv_total - tan_sum * attended
            attn_estimate = attn_estimate + jnp.sum(tan_out * head_parts(out_back, head), axis=1)

        attended = jnp.concatenate(attended_heads, axis=1)
        attended = attended.reshape(groups, 2, half, head_width)[:, 0].reshape(groups * half, head_width)

        pre_hidden = dot(normed, up_own)
        pre_own = pre_hidden.reshape(ctx_size, 2, half, units)[:, 0].reshape(ctx_size * half, units)
        hidden = jax.nn.gelu(pre_own, approximate=True).astype(BF16)
        near = dot(attended, out_own) + dot(hidden[:groups * half], down_own)
        parts = [near[k * half:(k + 1) * half] for k in range(groups)]
        if groups < ctx_size:
            far = dot(hidden[groups * half:], down_own)
            parts += [far[k * half:(k + 1) * half] for k in range(ctx_size - groups)]
        branch = sum_tp(ring_reduce(parts, cycle, BF16).astype(BF16))
        rows = rows + step_size * (gate * branch)

        dpre = tangent(pre_hidden, up_sign, up_pair, tokens)
        _, dhidden = jax.jvp(lambda u: jax.nn.gelu(u, approximate=True), (pre_hidden,), (dpre,))
        estimate = estimate + jnp.sum(dhidden * down_back, axis=1)
        estimate = estimate + jnp.pad(attn_estimate, (0, tokens - query_rows))

    lat_cols = lax.dynamic_slice_in_dim(rows, tp_index * local_width, local_width, 1)
    latent_out = join_probe(lat_cols, 0)

    by_slot = estimate.reshape(ctx_size, 2, half)
    by_slot = jnp.where(first, by_slot, by_slot[:, ::-1]).reshape(ctx_size, row_count)
    by_slot = jnp.concatenate([by_slot, jnp.zeros_like(by_slot)], axis=1)
    own_estimate = ring_reduce([by_slot[k:k + 1] for k in range(ctx_size)], cycle, F32)[:, :row_count]
    own_estimate = own_estimate + swap(own_estimate, "probe")
    own_estimate = sum_tp(own_estimate)[0]
    density_change = -step_size * own_estimate / (2 * math.sqrt(full_width))
    return (latent_out, density_change)


def solution(mesh):
    return jax.shard_map(
        local,
        mesh=mesh,
        in_specs=(
            P("ctx", "tp"),
            P("probe", "ctx", "tp"),
            P(),
            P("ctx", None),
            P(None, None, "tp"),
            P("tp", None),
            P("ctx", "tp"),
            P("tp", "ctx"),
            P("tp"),
            P("tp"),
        ),
        out_specs=(P("ctx", "tp"), P("ctx")),
        check_vma=False,
    )
```

```python
import math

import jax
import jax.numpy as jnp
from jax import lax
from jax.experimental import pallas as pl
from jax.experimental.pallas import tpu as pltpu
from jax.sharding import PartitionSpec as P

HD = 128
BLK = 128
STEPS = 2
EPS = 1e-06
NEG_BIG = -1e30
F32 = jnp.float32
BF16 = jnp.bfloat16


def after(value, *others):
    return lax.optimization_barrier((value,) + others)[0]


def dot(a, b):
    return jnp.dot(a, b, preferred_element_type=F32)


def dot_t(a, b):
    return lax.dot_general(a, b, (((1,), (1,)), ((), ())), preferred_element_type=F32)


def cycle_of(size):
    return list(range(0, size, 2)) + list(range(size - 1, 0, -2))


def ring_shift(x, cycle, shift):
    size = len(cycle)
    pairs = [(cycle[i], cycle[(i + shift) % size]) for i in range(size)]
    return lax.ppermute(x, "ctx", pairs)


def ring_gather(own, cycle, split_axis, jobs=()):
    size = len(cycle)
    reach = size // 2
    slots = [None] * size
    slots[0] = own
    fore = back = own
    jobs = list(jobs)
    for hop in range(1, reach):
        new_back = ring_shift(back, cycle, 1)
        new_fore = ring_shift(fore, cycle, -1)
        done = jobs.pop(0)(back) if jobs else []
        slots[size - hop], slots[hop] = new_back, new_fore
        back, fore = after(new_back, *done), after(new_fore, *done)
    first = ring_shift(jnp.split(back, 2, axis=split_axis)[0], cycle, 1)
    second = ring_shift(jnp.split(fore, 2, axis=split_axis)[1], cycle, -1)
    done = jobs.pop(0)(back) if jobs else []
    slots[reach] = after(jnp.concatenate([first, second], axis=split_axis), *done)
    while jobs:
        jobs.pop(0)(slots[reach])
    return slots


def ring_reduce(parts, cycle, wire, jobs=()):
    size = len(cycle)
    reach = size // 2
    width = parts[0].shape[1] // 2
    jobs = list(jobs)
    far = parts[reach].astype(wire)
    up = ring_shift(far[:, :width], cycle, 1)
    down = ring_shift(far[:, width:], cycle, -1)
    done = jobs.pop(0)(far) if jobs else []
    up, down = after(up, *done).astype(F32), after(down, *done).astype(F32)
    for hop in range(reach - 1, 0, -1):
        up_part, down_part = parts[hop], parts[size - hop]
        if hop == reach - 1:
            up = jnp.concatenate([up_part[:, :width] + up, up_part[:, width:].astype(F32)], axis=1)
            down = jnp.concatenate([down_part[:, :width].astype(F32), down_part[:, width:] + down], axis=1)
        else:
            up = up_part + up
            down = down_part + down
        up, down = up.astype(wire), down.astype(wire)
        new_up, new_down = ring_shift(up, cycle, 1), ring_shift(down, cycle, -1)
        done = jobs.pop(0)(up) if jobs else []
        up, down = after(new_up, *done).astype(F32), after(new_down, *done).astype(F32)
    while jobs:
        jobs.pop(0)(up)
    return parts[0] + up + down


def swap(x, axis):
    return lax.ppermute(x, axis, [(0, 1), (1, 0)])


def join_tp(own, axis):
    if lax.axis_size("tp") == 2:
        other = swap(own, "tp")
        first = lax.axis_index("tp") == 0
        low = jnp.where(first, own, other)
        high = jnp.where(first, other, own)
        return jnp.concatenate([low, high], axis=axis)
    return lax.all_gather(own, "tp", axis=axis, tiled=True)


def sum_tp(own):
    if lax.axis_size("tp") == 2:
        return own.astype(F32) + swap(own, "tp").astype(F32)
    return jnp.sum(lax.all_gather(own, "tp", axis=0, tiled=False).astype(F32), axis=0)


def join_probe(own, axis):
    other = swap(own, "probe")
    first = lax.axis_index("probe") == 0
    return jnp.concatenate([jnp.where(first, own, other), jnp.where(first, other, own)], axis=axis)


def assemble(pieces, places, shape, tail, offset):
    count = len(places)

    def kernel(offset_ref, *refs):
        ins, out = refs[:len(pieces)], refs[len(pieces)]
        sems = refs[-1]
        base = offset_ref[0]
        copies = []
        for index, (piece, start, height, row, side) in enumerate(places):
            source = ins[piece]
            width = pieces[piece].shape[1]
            if tail and side != "other":
                width -= tail
                copies.append(
                    pltpu.make_async_copy(
                        source.at[pl.ds(start, height), pl.ds(width, tail)],
                        refs[len(pieces) + 1].at[pl.ds(row, height), :],
                        sems.at[count + index],
                    )
                )
            if side == "all":
                target = out.at[pl.ds(row, height), :]
            else:
                column = pl.multiple_of(base if side == "own" else shape[1] - width - base, 128)
                target = out.at[pl.ds(row, height), pl.ds(column, width)]
            main = source.at[pl.ds(start, height), pl.ds(0, width)]
            copies.append(pltpu.make_async_copy(main, target, sems.at[index]))
        for copy in copies:
            copy.start()
        for copy in copies:
            copy.wait()

    size = pieces[0].dtype.itemsize * shape[0] * (shape[1] + tail)
    shapes = [jax.ShapeDtypeStruct(shape, pieces[0].dtype)]
    if tail:
        shapes.append(jax.ShapeDtypeStruct((shape[0], tail), pieces[0].dtype))
    outs = pl.pallas_call(
        kernel,
        out_shape=shapes,
        in_specs=[pl.BlockSpec(memory_space=pltpu.SMEM)] + [pl.BlockSpec(memory_space=pl.ANY)] * len(pieces),
        out_specs=[pl.BlockSpec(memory_space=pltpu.VMEM)] * len(shapes),
        scratch_shapes=[pltpu.SemaphoreType.DMA((2 * count if tail else count,))],
        compiler_params=pltpu.CompilerParams(vmem_limit_bytes=size + 4 * 1024 * 1024),
        cost_estimate=pl.CostEstimate(flops=0, bytes_accessed=2 * size, transcendentals=0),
    )(offset, *pieces)
    return outs if tail else outs[0]


def place_units(own, twin, probe, which):
    size, _, high, wide = own.shape
    shape = (2 * size * high, wide) if which == 0 else (2 * high, size * wide)

    def kernel(probe_ref, own_ref, twin_ref, out, sems):
        me = probe_ref[0]
        copies = []
        for ref, part in ((own_ref, me), (twin_ref, 1 - me)):
            for c in range(size):
                if which == 0:
                    start = pl.multiple_of((2 * c + part) * high, high)
                    target = out.at[pl.ds(start, high), :]
                else:
                    start = pl.multiple_of(part * high, high)
                    target = out.at[pl.ds(start, high), pl.ds(c * wide, wide)]
                copies.append(pltpu.make_async_copy(ref.at[c, which], target, sems.at[len(copies)]))
        for copy in copies:
            copy.start()
        for copy in copies:
            copy.wait()

    size_bytes = own.dtype.itemsize * shape[0] * shape[1]
    return pl.pallas_call(
        kernel,
        out_shape=jax.ShapeDtypeStruct(shape, own.dtype),
        in_specs=[pl.BlockSpec(memory_space=pltpu.SMEM)] + [pl.BlockSpec(memory_space=pl.ANY)] * 2,
        out_specs=pl.BlockSpec(memory_space=pltpu.VMEM),
        scratch_shapes=[pltpu.SemaphoreType.DMA((2 * size,))],
        compiler_params=pltpu.CompilerParams(vmem_limit_bytes=size_bytes + 4 * 1024 * 1024),
        cost_estimate=pl.CostEstimate(flops=0, bytes_accessed=2 * size_bytes, transcendentals=0),
    )(probe, own, twin)


def sign_products(parts, starts, scale, weights):
    tokens = parts[0].shape[0]
    width = weights[0].shape[0]
    widths = [weight.shape[1] for weight in weights]
    count = len(weights)
    block = 256 if tokens % 256 == 0 else tokens

    def kernel(starts_ref, scale_ref, *refs):
        outs = refs[count + len(parts):]
        totals = [None] * count
        for index, part_ref in enumerate(refs[count:count + len(parts)]):
            span = pl.ds(pl.multiple_of(starts_ref[index], 128), part_ref.shape[1])
            scaled = part_ref[...] * scale_ref[:, span]
            for at in range(count):
                product = dot(scaled, refs[at][span, :])
                totals[at] = product if index == 0 else totals[at] + product
        for total, out_ref in zip(totals, outs):
            out_ref[...] = total.astype(BF16)

    return pl.pallas_call(
        kernel,
        grid=(tokens // block,),
        out_shape=[jax.ShapeDtypeStruct((tokens, columns), BF16) for columns in widths],
        in_specs=[pl.BlockSpec(memory_space=pltpu.SMEM), pl.BlockSpec((1, width), lambda i: (0, 0))]
        + [pl.BlockSpec(weight.shape, lambda i: (0, 0)) for weight in weights]
        + [pl.BlockSpec((block, part.shape[1]), lambda i: (i, 0)) for part in parts],
        out_specs=[pl.BlockSpec((block, columns), lambda i: (i, 0)) for columns in widths],
        compiler_params=pltpu.CompilerParams(vmem_limit_bytes=48 * 1024 * 1024),
        cost_estimate=pl.CostEstimate(
            flops=2 * tokens * width * sum(widths),
            bytes_accessed=2 * (tokens * width + width * sum(widths) + tokens * sum(widths)),
            transcendentals=0,
        ),
    )(starts, scale, *weights, *parts)


def lanes_of(values, count):
    lane = lax.broadcasted_iota(jnp.int32, (values[0].shape[0], count), 1)
    tile = jnp.zeros(lane.shape, F32)
    for index, value in enumerate(values):
        tile = jnp.where(lane == index, value, tile)
    return tile


def row_sums(rows, own_sign, twin_sign):
    total = [jnp.sum(rows, axis=1, keepdims=True), jnp.sum(rows * rows, axis=1, keepdims=True)]
    for sign in (own_sign.astype(F32), twin_sign.astype(F32)):
        total += [jnp.sum(sign, axis=1, keepdims=True), jnp.sum(rows * sign, axis=1, keepdims=True)]
    return total


def partial_sums(rows, own_sign, twin_sign):
    def kernel(rows_ref, own_ref, twin_ref, out_ref):
        out_ref[...] = lanes_of(row_sums(rows_ref[...], own_ref[...], twin_ref[...]), 128)

    return pl.pallas_call(kernel, out_shape=jax.ShapeDtypeStruct((rows.shape[0], 128), F32))(
        rows, own_sign, twin_sign
    )


def write_packet(packet_ref, rows, sums, mod, lists, full_width):
    width = rows.shape[1]
    means = [value / full_width for value in sums]
    inv_std = lax.rsqrt(means[1] - means[0] * means[0] + EPS)
    unit_rows = (rows - means[0]) * inv_std
    packet_ref[:, 0:width] = (unit_rows * (1.0 + mod[1:2]) + mod[0:1]).astype(BF16)
    scalars = [inv_std]
    for index in (2, 4):
        scalars += [means[index], (means[index + 1] - means[0] * means[index]) * inv_std]
    high = [value.astype(BF16).astype(F32) for value in scalars]
    low = [value - part for value, part in zip(scalars, high)]
    tail = lanes_of(high + low, 128) + lists.astype(F32)
    packet_ref[:, width:width + 128] = tail.astype(BF16)


def first_packet(rows, sums_own, sums_other, mod, lists, full_width):
    def kernel(rows_ref, own_ref, other_ref, mod_ref, lists_ref, packet_ref):
        sums = own_ref[...] + other_ref[...]
        sums = [sums[:, i:i + 1] for i in range(6)]
        write_packet(packet_ref, rows_ref[...], sums, mod_ref[...], lists_ref[...], full_width)

    height, width = rows.shape
    return pl.pallas_call(kernel, out_shape=jax.ShapeDtypeStruct((height, width + 128), BF16))(
        rows, sums_own, sums_other, mod, lists
    )


def next_packet(rows, branch_own, branch_other, gate, own_sign, twin_sign, mod, lists, step_size):
    def kernel(rows_ref, own_ref, other_ref, gate_ref, own_sign_ref, twin_sign_ref, mod_ref, lists_ref,
               new_ref, packet_ref):
        branch = own_ref[...].astype(F32) + other_ref[...].astype(F32)
        new = rows_ref[...] + step_size * (gate_ref[...] * branch)
        new_ref[...] = new
        sums = row_sums(new, own_sign_ref[...], twin_sign_ref[...])
        write_packet(packet_ref, new, sums, mod_ref[...], lists_ref[...], new.shape[1])

    height, width = rows.shape
    return pl.pallas_call(
        kernel,
        out_shape=[
            jax.ShapeDtypeStruct((height, width), F32),
            jax.ShapeDtypeStruct((height, width + 128), BF16),
        ],
        compiler_params=pltpu.CompilerParams(vmem_limit_bytes=24 * 1024 * 1024),
    )(rows, branch_own, branch_other, gate, own_sign, twin_sign, mod, lists)


def token_scalars(tails, own_half):
    sums = tails[:, 0:5].astype(F32) + tails[:, 5:10].astype(F32)
    if own_half:
        return sums[:, 0:1], sums[:, 1:2], sums[:, 2:3]
    return sums[:, 0:1], sums[:, 3:4], sums[:, 4:5]


def mlp_tangent(pre_hidden, sign, consts, tails, back):
    tokens, units = sign.shape
    half = tokens // 2
    lanes = HD if units % HD == 0 else units

    def kernel(own_ref, twin_ref, sign_ref, const_ref, own_tail_ref, twin_tail_ref, back_ref, out_ref):
        for part, pre_ref, tail_ref in ((0, own_ref, own_tail_ref), (1, twin_ref, twin_tail_ref)):
            rows = pl.ds(part * half, half)
            inv, mean, cross = token_scalars(tail_ref[...], part == 0)
            pre = pre_ref[...]
            tan = inv * (sign_ref[rows, :].astype(F32) - mean * const_ref[0:1] - cross * (pre - const_ref[1:2]))
            inner = math.sqrt(2.0 / math.pi) * (pre + 0.044715 * (pre * pre * pre))
            bend = jnp.tanh(inner)
            slope = math.sqrt(2.0 / math.pi) * (1.0 + 3.0 * 0.044715 * (pre * pre))
            gelu_slope = 0.5 * (1.0 + bend) + 0.5 * pre * (1.0 - bend * bend) * slope
            product = gelu_slope * tan * back_ref[rows, :].astype(F32)
            out_ref[rows, :] = sum(product[:, i:i + lanes] for i in range(0, units, lanes))

    return pl.pallas_call(
        kernel,
        out_shape=jax.ShapeDtypeStruct((tokens, lanes), F32),
        compiler_params=pltpu.CompilerParams(vmem_limit_bytes=48 * 1024 * 1024),
        cost_estimate=pl.CostEstimate(
            flops=6000 * tokens * units, bytes_accessed=10 * tokens * units, transcendentals=tokens * units
        ),
    )(pre_hidden[0], pre_hidden[1], sign, consts, tails[0], tails[1], back)


def normed_head(raw, gain):
    inv = lax.rsqrt(jnp.mean(raw * raw, axis=1, keepdims=True) + EPS)
    return (raw * inv * gain).astype(BF16), inv


def attention(raw_own, raw_twin, bias, q_gain, k_gain, heads):
    queries, tokens = bias.shape
    half = tokens // 2
    scale = 1.0 / math.sqrt(HD)

    def kernel(q_ref, k_ref, v_ref, k_twin_ref, v_twin_ref, bias_ref, qg_ref, kg_ref, out_ref):
        q_n, _ = normed_head(q_ref[...], qg_ref[...])
        k_n = jnp.concatenate(
            [normed_head(k_ref[...], kg_ref[...])[0], normed_head(k_twin_ref[...], kg_ref[...])[0]], axis=0
        )
        v_n = jnp.concatenate([v_ref[...].astype(BF16), v_twin_ref[...].astype(BF16)], axis=0)
        scores = dot_t(q_n, k_n) * scale + bias_ref[...]
        weights = jnp.exp(scores - jnp.max(scores, axis=1, keepdims=True))
        total = jnp.sum(weights, axis=1, keepdims=True)
        out_ref[...] = (dot(weights.astype(BF16), v_n) / total).astype(BF16)

    def columns(part, height):
        return pl.BlockSpec((height, HD), lambda h: (0, part * heads + h))

    return pl.pallas_call(
        kernel,
        grid=(heads,),
        out_shape=jax.ShapeDtypeStruct((queries, heads * HD), BF16),
        in_specs=[
            columns(0, queries),
            columns(1, half),
            columns(2, half),
            columns(1, half),
            columns(2, half),
            pl.BlockSpec((queries, tokens), lambda h: (0, 0)),
            columns(0, 1),
            columns(0, 1),
        ],
        out_specs=columns(0, queries),
        compiler_params=pltpu.CompilerParams(vmem_limit_bytes=32 * 1024 * 1024),
        cost_estimate=pl.CostEstimate(
            flops=30 * heads * queries * tokens * HD,
            bytes_accessed=12 * heads * tokens * HD + 4 * queries * tokens,
            transcendentals=heads * queries * tokens,
        ),
    )(raw_own, raw_own, raw_own, raw_twin, raw_twin, bias, q_gain, k_gain)


def attention_tangent(
    raw, sign, consts, tails, back, bias, q_gain, k_gain, heads
):
    queries, tokens = bias.shape
    scale = 1.0 / math.sqrt(HD)
    half = tokens // 2

    def kernel(q_ref, k_ref, v_ref, q_twin_ref, k_twin_ref, v_twin_ref, qs_ref, ks_ref, vs_ref, qc_ref, kc_ref,
               vc_ref, tail_ref, tail_twin_ref, back_ref, bias_ref, qg_ref, kg_ref, out_ref):
        head = pl.program_id(0)
        own = token_scalars(tail_ref[...], True)
        twin = token_scalars(tail_twin_ref[...], False)
        every = [jnp.concatenate(pair, axis=0) for pair in zip(own, twin)]

        def tangent(raw_rows, sign_rows, const_ref, columns):
            inv, mean, cross = columns
            return inv * (
                sign_rows.astype(F32) - mean * const_ref[0:1] - cross * (raw_rows - const_ref[1:2])
            )

        def tangent_head(raw_rows, tan, inv, gain):
            tan_inv = -inv * inv * inv * jnp.mean(raw_rows * tan, axis=1, keepdims=True)
            return ((tan * inv + raw_rows * tan_inv) * gain).astype(BF16)

        k_raw = jnp.concatenate([k_ref[...], k_twin_ref[...]], axis=0)
        k_n, k_inv = normed_head(k_raw, kg_ref[...])
        dk_n = tangent_head(k_raw, tangent(k_raw, ks_ref[...], kc_ref, every), k_inv, kg_ref[...])
        keys = jnp.concatenate([k_n, dk_n], axis=1)
        v_raw = jnp.concatenate([v_ref[...], v_twin_ref[...]], axis=0)
        v_n = v_raw.astype(BF16)
        values = jnp.concatenate([v_n, tangent(v_raw, vs_ref[...], vc_ref, every).astype(BF16)], axis=1)
        for part in range(2):
            q_raw = (q_twin_ref if part else q_ref)[...]
            rows = pl.ds(part * half, queries)
            q_n, q_inv = normed_head(q_raw, qg_ref[...])
            columns = [column[:queries] for column in (twin if part else own)]
            dq_n = tangent_head(q_raw, tangent(q_raw, qs_ref[rows, :], qc_ref, columns), q_inv, qg_ref[...])
            scores = dot_t(q_n, k_n) * scale + bias_ref[...]
            weights = jnp.exp(scores - jnp.max(scores, axis=1, keepdims=True))
            inv_total = 1.0 / jnp.sum(weights, axis=1, keepdims=True)
            weighted = weights * (dot_t(jnp.concatenate([dq_n, q_n], axis=1), keys) * scale)
            tan_sum = jnp.sum(weighted, axis=1, keepdims=True) * inv_total
            both = dot(weights.astype(BF16), values) * inv_total
            tan_out = both[:, HD:] + dot(weighted.astype(BF16), v_n) * inv_total - tan_sum * both[:, :HD]
            share = tan_out * back_ref[rows, :].astype(F32)
            span = pl.ds(part * queries, queries)

            @pl.when(head == 0)
            def _():
                out_ref[span, :] = share

            @pl.when(head > 0)
            def _():
                out_ref[span, :] += share

    def columns(part, height):
        return pl.BlockSpec((height, HD), lambda i: (0, part * heads + i))

    def whole(array):
        return pl.BlockSpec(array.shape, lambda i: (0, 0))

    return pl.pallas_call(
        kernel,
        grid=(heads,),
        out_shape=jax.ShapeDtypeStruct((2 * queries, HD), F32),
        in_specs=[columns(0, queries), columns(1, half), columns(2, half)] * 2
        + [columns(i, tokens) for i in range(3)]
        + [columns(i, consts.shape[0]) for i in range(3)]
        + [whole(tails[0]), whole(tails[1]), columns(0, tokens), whole(bias), columns(0, 1), columns(0, 1)],
        out_specs=pl.BlockSpec((2 * queries, HD), lambda i: (0, 0)),
        compiler_params=pltpu.CompilerParams(vmem_limit_bytes=48 * 1024 * 1024),
        cost_estimate=pl.CostEstimate(
            flops=140 * heads * queries * tokens * HD,
            bytes_accessed=32 * heads * tokens * HD + 4 * queries * tokens,
            transcendentals=2 * heads * queries * tokens,
        ),
    )(
        *[raw[0]] * 3, *[raw[1]] * 3, sign, sign, sign, consts, consts, consts, tails[0], tails[1], back, bias,
        q_gain, k_gain,
    )


def local(latent, probes, modulation, pattern, w_qkv, w_out, w_up, w_down, q_gain, k_gain):
    ctx_size = lax.axis_size("ctx")
    tp_size = lax.axis_size("tp")
    cycle = cycle_of(ctx_size)
    row_count, local_width = latent.shape
    half = row_count // 2
    full_width = local_width * tp_size
    tokens = row_count * ctx_size
    heads_local = q_gain.shape[0] // HD
    groups = math.gcd(heads_local, ctx_size)
    heads_own = heads_local // groups
    head_width = heads_own * HD
    queries = groups * half
    unit_total = w_up.shape[1]
    units = unit_total // ctx_size
    list_size = pattern.shape[1]
    step_size = 1.0 / STEPS

    ctx_index = lax.axis_index("ctx")
    probe_index = lax.axis_index("probe")
    tp_index = lax.axis_index("tp")
    first = probe_index == 0
    cycle_arr = jnp.array(cycle, jnp.int32)
    place = jnp.array([cycle.index(i) for i in range(ctx_size)], jnp.int32)
    ring_index = place[ctx_index]
    slot_owner = cycle_arr[(ring_index + jnp.arange(ctx_size)) % ctx_size]
    owner_slot = (place - ring_index) % ctx_size
    group = ring_index % groups
    column_offset = (tp_index * local_width).astype(jnp.int32).reshape(1)

    signs_local = (2 * probes[0] - 1).astype(BF16).reshape(2, half, local_width)
    signs_local = jnp.where(first, signs_local, signs_local[::-1]).reshape(row_count, local_width)
    own_sign, twin_sign = signs_local[:half], swap(signs_local[half:], "probe")
    sign_slots = ring_gather(signs_local, cycle, 1)
    lat_half = lax.dynamic_slice_in_dim(latent, probe_index * half, half, 0)
    rows = join_tp(lat_half, 1)
    places = [
        (k, part * half, half, (part * ctx_size + k) * half, "own") for k in range(ctx_size) for part in range(2)
    ]
    signs = assemble(sign_slots, places, (tokens, local_width), 0, column_offset * 0)
    if tp_size == 2:
        sign_parts = [signs, swap(signs, "tp")]
        sign_starts = jnp.concatenate([column_offset, local_width - column_offset])
        low = tp_index == 0
        block_signs = [
            jnp.concatenate([jnp.where(low, own, other), jnp.where(low, other, own)], axis=1)
            for own, other in ([part[at:at + half] for part in sign_parts] for at in (0, tokens // 2))
        ]
    else:
        sign_parts = [lax.all_gather(signs, "tp", axis=1, tiled=True)]
        sign_starts = column_offset * 0
        block_signs = [sign_parts[0][at:at + half] for at in (0, tokens // 2)]
    own_signs, twin_signs = block_signs[0], swap(block_signs[1], "probe")

    qkv_own = lax.dynamic_slice_in_dim(w_qkv, group * head_width, head_width, 2)
    qkv_own = after(jnp.concatenate([qkv_own[:, part] for part in range(3)], axis=1))
    out_own = lax.dynamic_slice_in_dim(w_out, group * head_width, head_width, 0)
    q_gain_own = lax.dynamic_slice_in_dim(q_gain, group * head_width, head_width, 0)[None]
    k_gain_own = lax.dynamic_slice_in_dim(k_gain, group * head_width, head_width, 0)[None]

    stretches = (1.0 + modulation[:, 1]).astype(BF16)
    gates = modulation[:, 2].astype(BF16)
    lists = jnp.pad(pattern.astype(BF16), ((0, 0), (10, 128 - 10 - list_size)))

    half_tokens = ctx_size * half
    out_turned = out_own.T

    def products(step, back):
        def job(token):
            scale = after((gates if back else stretches)[step][None], token)
            weights = [out_turned, down_turned] if back else [qkv_own, up_own]
            if step == 0:
                made = [early[back]] + list(sign_products(sign_parts, sign_starts, scale, weights[1:]))
            else:
                made = sign_products(sign_parts, sign_starts, scale, weights)
            found[step, back] = made
            return made

        return job

    def head_tangent(step):
        def job(token):
            raw, tails, pre, pairs = kept[step]
            share = attention_tangent(
                (after(raw[0], token), raw[1]), found[step, False][0], pairs[0], tails, found[step, True][0],
                bias, q_gain_own, k_gain_own, heads_own,
            )
            attn_shares.append(share)
            return [share]

        return job

    def unit_tangent(step):
        def job(token):
            raw, tails, pre, pairs = kept[step]
            pre_twin = dot(after(pre[1], token), up_own)
            share = mlp_tangent(
                (pre[0], pre_twin), found[step, False][1], pairs[1], tails, found[step, True][1]
            )
            mlp_shares.append(share)
            return [share]

        return job

    def no_job(token):
        return []

    found = {}
    kept, attn_shares, mlp_shares = [], [], []

    bias = None
    for step in range(STEPS):
        mod = modulation[step]
        shift, stretch, gate = mod[0][None], 1.0 + mod[1][None], mod[2][None]

        if step == 0:
            sums = partial_sums(lat_half, own_sign, twin_sign)
            if tp_size == 2:
                sums_other = swap(sums, "tp")
            else:
                sums_other = lax.psum(sums, "tp") - sums
            packet = first_packet(rows, sums, sums_other, mod, lists, full_width)
            slots = ring_gather(packet, cycle, 0)
            at = slots[0].shape[1] - 128 + 10
            listed = jnp.stack([slots[k][0, at:at + list_size] for k in range(groups)]).astype(jnp.int32)
            listed = jnp.any(listed[:, :, None] == slot_owner[None, None, :], axis=1)
            bias = jnp.where(listed, 0.0, NEG_BIG).astype(F32)
            bias = jnp.tile(jnp.repeat(jnp.repeat(bias, half, axis=0), half, axis=1), (1, 2))
        else:
            rows, packet = next_packet(
                rows, branch, branch_other, last_gate, own_signs, twin_signs, mod, lists, step_size
            )
            jobs = [head_tangent(step - 1), no_job, unit_tangent(step - 1)]
            slots = ring_gather(packet, cycle, 0, jobs)
        places = [(k, 0, half, k * half, "all") for k in range(ctx_size)]
        normed, tails = assemble(slots, places, (half_tokens, full_width), 128, column_offset)

        normed_twin, tails_twin = swap(normed, "probe"), swap(tails, "probe")
        raw_own = dot(normed, qkv_own)
        if step == 0:
            raw_twin = dot(normed_twin, qkv_own)
            attended = attention(raw_own, raw_twin, bias, q_gain_own, k_gain_own, heads_own)

            early = [
                sign_products(sign_parts, sign_starts, after(scales[0][None], attended), [weight])[0]
                for scales, weight in ((stretches, qkv_own), (gates, out_turned))
            ]
            up_late, down_late = after(w_up, slots[ctx_size // 2], signs), after(w_down, slots[ctx_size // 2], signs)
            up_part = lax.dynamic_slice_in_dim(up_late, probe_index * (w_up.shape[0] // 2), w_up.shape[0] // 2, 0)
            up_part = up_part.reshape(-1, ctx_size, units).transpose(1, 0, 2)
            down_part = down_late.reshape(ctx_size, 2, units // 2, w_down.shape[1])
            down_part = lax.dynamic_index_in_dim(down_part, probe_index, 1, keepdims=False)
            fused = up_part.shape == down_part.shape
            if fused:
                got = lax.all_to_all(jnp.stack([up_part, down_part], axis=1), "ctx", 0, 0, tiled=True)
                got = after(got, attended, *early)
                got_twin = swap(got, "probe")
                core = probe_index.astype(jnp.int32).reshape(1)
                up_own = place_units(got, got_twin, core, 0)
                down_own = place_units(got, got_twin, core, 1)
            else:
                got = lax.all_to_all(up_part, "ctx", 0, 0, tiled=True)
                pair = jnp.stack([got, swap(got, "probe")], axis=1)
                up_own = jnp.where(first, pair, pair[:, ::-1]).reshape(full_width, units)
                got = lax.all_to_all(down_part, "ctx", 0, 0, tiled=True)
                down_own = join_probe(got.transpose(1, 0, 2).reshape(units // 2, full_width), 0)
            down_turned = down_own.T

        pre_own = dot(normed, up_own)
        hidden = jax.nn.gelu(pre_own, approximate=True).astype(BF16)
        parts = []
        if groups < ctx_size:
            far = dot(hidden[queries:], down_own)
            parts = [far[k * half:(k + 1) * half] for k in range(ctx_size - groups)]
        if step > 0:
            raw_twin = dot(normed_twin, qkv_own)
            attended = attention(raw_own, raw_twin, bias, q_gain_own, k_gain_own, heads_own)
        near = dot(attended, out_own) + dot(hidden[:queries], down_own)
        parts = [near[k * half:(k + 1) * half] for k in range(groups)] + parts

        pair = jnp.concatenate(
            [stretches[step][None], shift.astype(BF16), jnp.zeros((14, full_width), BF16)], axis=0
        )
        pairs = (dot(pair, qkv_own), dot(pair, up_own))
        kept.append(((raw_own, raw_twin), (tails, tails_twin), (pre_own, normed_twin), pairs))
        if step == 0:
            jobs = [products(0, False), products(0, True), products(1, False), products(1, True)]
        else:
            jobs = [no_job, head_tangent(step), no_job, unit_tangent(step)]
        branch = ring_reduce(parts, cycle, BF16, jobs).astype(BF16)
        if tp_size == 2:
            branch_other = swap(branch, "tp")
        else:
            branch_other = sum_tp(branch) - branch.astype(F32)
        last_gate = gate

    rows = rows + step_size * (last_gate * (branch.astype(F32) + branch_other.astype(F32)))
    estimate = jnp.sum(sum(mlp_shares), axis=1)
    attn_share = jnp.sum(sum(attn_shares), axis=1).reshape(2, queries)
    estimate = estimate + jnp.pad(attn_share, ((0, 0), (0, half_tokens - queries))).reshape(tokens)
    lat_cols = lax.dynamic_slice_in_dim(rows, tp_index * local_width, local_width, 1)
    latent_out = join_probe(lat_cols, 0)

    by_slot = estimate.reshape(2, ctx_size, half)
    by_slot = jnp.where(first, by_slot, by_slot[::-1]).transpose(1, 0, 2).reshape(ctx_size, row_count)
    by_slot = jnp.concatenate([by_slot, jnp.zeros_like(by_slot)], axis=1)
    own_estimate = ring_reduce([by_slot[k:k + 1] for k in range(ctx_size)], cycle, F32)[:, :row_count]
    own_estimate = own_estimate + swap(own_estimate, "probe")
    own_estimate = sum_tp(own_estimate)[0]
    density_change = -step_size * own_estimate / (2 * math.sqrt(full_width))
    return (latent_out, density_change)


def solution(mesh):
    return jax.shard_map(
        local,
        mesh=mesh,
        in_specs=(
            P("ctx", "tp"),
            P("probe", "ctx", "tp"),
            P(),
            P("ctx", None),
            P(None, None, "tp"),
            P("tp", None),
            P("ctx", "tp"),
            P("tp", "ctx"),
            P("tp"),
            P("tp"),
        ),
        out_specs=(P("ctx", "tp"), P("ctx")),
        check_vma=False,
    )
```

```python
import math

import jax
import jax.numpy as jnp
from jax import lax
from jax.experimental import pallas as pl
from jax.experimental.pallas import tpu as pltpu
from jax.sharding import PartitionSpec as P

HD = 128
BLK = 128
STEPS = 2
EPS = 1e-06
NEG_BIG = -1e30
F32 = jnp.float32
BF16 = jnp.bfloat16


def after(value, *others):
    return lax.optimization_barrier((value,) + others)[0]


def dot(a, b):
    return jnp.dot(a, b, preferred_element_type=F32)


def dot_t(a, b):
    return lax.dot_general(a, b, (((1,), (1,)), ((), ())), preferred_element_type=F32)


def cycle_of(size):
    return list(range(0, size, 2)) + list(range(size - 1, 0, -2))


def ring_shift(x, cycle, shift):
    size = len(cycle)
    pairs = [(cycle[i], cycle[(i + shift) % size]) for i in range(size)]
    return lax.ppermute(x, "ctx", pairs)


def ring_gather(own, cycle, split_axis, jobs=()):
    size = len(cycle)
    reach = size // 2
    slots = [None] * size
    slots[0] = own
    fore = back = own
    jobs = list(jobs)
    for hop in range(1, reach):
        new_back = ring_shift(back, cycle, 1)
        new_fore = ring_shift(fore, cycle, -1)
        done = jobs.pop(0)(back) if jobs else []
        slots[size - hop], slots[hop] = new_back, new_fore
        back, fore = after(new_back, *done), after(new_fore, *done)
    first = ring_shift(jnp.split(back, 2, axis=split_axis)[0], cycle, 1)
    second = ring_shift(jnp.split(fore, 2, axis=split_axis)[1], cycle, -1)
    done = jobs.pop(0)(back) if jobs else []
    slots[reach] = after(jnp.concatenate([first, second], axis=split_axis), *done)
    return slots[-1:] + slots[:-1]


def ring_reduce(parts, cycle, wire, jobs=()):
    size = len(cycle)
    reach = size // 2
    parts = parts[1:] + parts[:1]
    width = parts[0].shape[1] // 2
    jobs = list(jobs)
    far = parts[reach].astype(wire)
    up = ring_shift(far[:, :width], cycle, 1)
    down = ring_shift(far[:, width:], cycle, -1)
    done = jobs.pop(0)(far) if jobs else []
    up, down = after(up, *done).astype(F32), after(down, *done).astype(F32)
    for hop in range(reach - 1, 0, -1):
        up_part, down_part = parts[hop], parts[size - hop]
        if hop == reach - 1:
            up = jnp.concatenate([up_part[:, :width] + up, up_part[:, width:].astype(F32)], axis=1)
            down = jnp.concatenate([down_part[:, :width].astype(F32), down_part[:, width:] + down], axis=1)
        else:
            up = up_part + up
            down = down_part + down
        up, down = up.astype(wire), down.astype(wire)
        new_up, new_down = ring_shift(up, cycle, 1), ring_shift(down, cycle, -1)
        done = jobs.pop(0)(up) if jobs else []
        up, down = after(new_up, *done).astype(F32), after(new_down, *done).astype(F32)
    return parts[0] + up + down


def swap(x, axis):
    return lax.ppermute(x, axis, [(0, 1), (1, 0)])


def join_tp(own, axis):
    if lax.axis_size("tp") == 2:
        other = swap(own, "tp")
        first = lax.axis_index("tp") == 0
        low = jnp.where(first, own, other)
        high = jnp.where(first, other, own)
        return jnp.concatenate([low, high], axis=axis)
    return lax.all_gather(own, "tp", axis=axis, tiled=True)


def sum_tp(own):
    if lax.axis_size("tp") == 2:
        return own.astype(F32) + swap(own, "tp").astype(F32)
    return jnp.sum(lax.all_gather(own, "tp", axis=0, tiled=False).astype(F32), axis=0)


def join_probe(own, axis):
    other = swap(own, "probe")
    first = lax.axis_index("probe") == 0
    return jnp.concatenate([jnp.where(first, own, other), jnp.where(first, other, own)], axis=axis)


def assemble(pieces, places, shape, tail, offset):
    count = len(places)

    def kernel(offset_ref, *refs):
        ins, out = refs[:len(pieces)], refs[len(pieces)]
        sems = refs[-1]
        base = offset_ref[0]
        copies = []
        for index, (piece, start, height, row, side) in enumerate(places):
            source = ins[piece]
            width = pieces[piece].shape[1]
            if tail and side != "other":
                width -= tail
                copies.append(
                    pltpu.make_async_copy(
                        source.at[pl.ds(start, height), pl.ds(width, tail)],
                        refs[len(pieces) + 1].at[pl.ds(row, height), :],
                        sems.at[count + index],
                    )
                )
            if side == "all":
                target = out.at[pl.ds(row, height), :]
            else:
                column = pl.multiple_of(base if side == "own" else shape[1] - width - base, 128)
                target = out.at[pl.ds(row, height), pl.ds(column, width)]
            main = source.at[pl.ds(start, height), pl.ds(0, width)]
            copies.append(pltpu.make_async_copy(main, target, sems.at[index]))
        for copy in copies:
            copy.start()
        for copy in copies:
            copy.wait()

    size = pieces[0].dtype.itemsize * shape[0] * (shape[1] + tail)
    shapes = [jax.ShapeDtypeStruct(shape, pieces[0].dtype)]
    if tail:
        shapes.append(jax.ShapeDtypeStruct((shape[0], tail), pieces[0].dtype))
    outs = pl.pallas_call(
        kernel,
        out_shape=shapes,
        in_specs=[pl.BlockSpec(memory_space=pltpu.SMEM)] + [pl.BlockSpec(memory_space=pl.ANY)] * len(pieces),
        out_specs=[pl.BlockSpec(memory_space=pltpu.VMEM)] * len(shapes),
        scratch_shapes=[pltpu.SemaphoreType.DMA((2 * count if tail else count,))],
        compiler_params=pltpu.CompilerParams(vmem_limit_bytes=size + 4 * 1024 * 1024),
        cost_estimate=pl.CostEstimate(flops=0, bytes_accessed=2 * size, transcendentals=0),
    )(offset, *pieces)
    return outs if tail else outs[0]


def place_units(own, twin, probe, which):
    size, _, high, wide = own.shape
    shape = (2 * size * high, wide) if which == 0 else (2 * high, size * wide)

    def kernel(probe_ref, own_ref, twin_ref, out, sems):
        me = probe_ref[0]
        copies = []
        for ref, part in ((own_ref, me), (twin_ref, 1 - me)):
            for c in range(size):
                if which == 0:
                    start = pl.multiple_of((2 * c + part) * high, high)
                    target = out.at[pl.ds(start, high), :]
                else:
                    start = pl.multiple_of(part * high, high)
                    target = out.at[pl.ds(start, high), pl.ds(c * wide, wide)]
                copies.append(pltpu.make_async_copy(ref.at[c, which], target, sems.at[len(copies)]))
        for copy in copies:
            copy.start()
        for copy in copies:
            copy.wait()

    size_bytes = own.dtype.itemsize * shape[0] * shape[1]
    return pl.pallas_call(
        kernel,
        out_shape=jax.ShapeDtypeStruct(shape, own.dtype),
        in_specs=[pl.BlockSpec(memory_space=pltpu.SMEM)] + [pl.BlockSpec(memory_space=pl.ANY)] * 2,
        out_specs=pl.BlockSpec(memory_space=pltpu.VMEM),
        scratch_shapes=[pltpu.SemaphoreType.DMA((2 * size,))],
        compiler_params=pltpu.CompilerParams(vmem_limit_bytes=size_bytes + 4 * 1024 * 1024),
        cost_estimate=pl.CostEstimate(flops=0, bytes_accessed=2 * size_bytes, transcendentals=0),
    )(probe, own, twin)


def sign_products(parts, starts, scales, weight, columns):
    tokens = parts[0].shape[0]
    width, total_columns = weight.shape
    blocks, steps, _ = scales.shape
    if columns % 128:
        made = []
        for step in range(steps):
            scaled = [(parts, scales[at, step][None], weight[:, at * columns:(at + 1) * columns]) for at in range(blocks)]
            made.append(jnp.concatenate([dot(signs[0] * scale, own) for signs, scale, own in scaled], axis=1))
        return jnp.stack(made).astype(BF16)

    def kernel(starts_ref, scale_ref, weight_ref, *refs):
        out_ref = refs[-1]
        spans = [
            pl.ds(pl.multiple_of(starts_ref[index], 128), part.shape[1]) for index, part in enumerate(parts)
        ]
        for step in range(steps):
            total = None
            for span, part_ref in zip(spans, refs):
                product = dot(part_ref[...] * scale_ref[0, step:step + 1, span], weight_ref[span, :])
                total = product if total is None else total + product
            out_ref[step] = total.astype(BF16)

    flops = 2 * steps * tokens * width * total_columns
    return pl.pallas_call(
        kernel,
        grid=(blocks,),
        out_shape=jax.ShapeDtypeStruct((steps, tokens, total_columns), BF16),
        in_specs=[
            pl.BlockSpec(memory_space=pltpu.SMEM),
            pl.BlockSpec((1, steps, width), lambda i: (i, 0, 0)),
            pl.BlockSpec((width, columns), lambda i: (0, i)),
        ]
        + [pl.BlockSpec(part.shape, lambda i: (0, 0)) for part in parts],
        out_specs=pl.BlockSpec((steps, tokens, columns), lambda i: (0, 0, i)),
        compiler_params=pltpu.CompilerParams(vmem_limit_bytes=32 * 1024 * 1024),
        cost_estimate=pl.CostEstimate(
            flops=flops + flops // 2,
            bytes_accessed=2 * (tokens * width + width * total_columns + steps * tokens * total_columns),
            transcendentals=0,
        ),
    )(starts, scales, weight, *parts)


def project(rows, weight, columns):
    tokens, width = rows.shape
    total_columns = weight.shape[1]

    def kernel(rows_ref, weight_ref, out_ref):
        out_ref[...] = dot(rows_ref[...], weight_ref[...])

    return pl.pallas_call(
        kernel,
        grid=(total_columns // columns,),
        out_shape=jax.ShapeDtypeStruct((tokens, total_columns), F32),
        in_specs=[
            pl.BlockSpec((tokens, width), lambda i: (0, 0)),
            pl.BlockSpec((width, columns), lambda i: (0, i)),
        ],
        out_specs=pl.BlockSpec((tokens, columns), lambda i: (0, i)),
        compiler_params=pltpu.CompilerParams(vmem_limit_bytes=24 * 1024 * 1024),
        cost_estimate=pl.CostEstimate(
            flops=3 * tokens * width * total_columns,
            bytes_accessed=2 * (tokens * width + width * total_columns) + 4 * tokens * total_columns,
            transcendentals=0,
        ),
    )(rows, weight)


def gelu_tanh(pre):
    inner = math.sqrt(2.0 / math.pi) * (pre + 0.044715 * (pre * pre * pre))
    return 0.5 * pre * (1.0 + jnp.tanh(inner))


def hidden_units(normed, up, down, first_far):
    tokens, width = normed.shape
    units = up.shape[1]

    def kernel(normed_ref, up_ref, down_ref, pre_ref, hidden_ref, far_ref):
        pre = dot(normed_ref[...], up_ref[...])
        pre_ref[...] = pre
        hidden = gelu_tanh(pre).astype(BF16)
        hidden_ref[...] = hidden[:first_far]
        far_ref[...] = dot(hidden[first_far:], down_ref[...]).astype(BF16)

    return pl.pallas_call(
        kernel,
        out_shape=[
            jax.ShapeDtypeStruct((tokens, units), F32),
            jax.ShapeDtypeStruct((first_far, units), BF16),
            jax.ShapeDtypeStruct((tokens - first_far, width), BF16),
        ],
        compiler_params=pltpu.CompilerParams(vmem_limit_bytes=28 * 1024 * 1024),
        cost_estimate=pl.CostEstimate(
            flops=4 * tokens * width * units,
            bytes_accessed=2 * (2 * tokens * width + 2 * width * units),
            transcendentals=tokens * units,
        ),
    )(normed, up, down)


def lanes_of(values, count):
    lane = lax.broadcasted_iota(jnp.int32, (values[0].shape[0], count), 1)
    tile = jnp.zeros(lane.shape, F32)
    for index, value in enumerate(values):
        tile = jnp.where(lane == index, value, tile)
    return tile


def row_sums(rows, own_sign, twin_sign):
    total = [jnp.sum(rows, axis=1, keepdims=True), jnp.sum(rows * rows, axis=1, keepdims=True)]
    for sign in (own_sign.astype(F32), twin_sign.astype(F32)):
        total += [jnp.sum(sign, axis=1, keepdims=True), jnp.sum(rows * sign, axis=1, keepdims=True)]
    return total


def partial_sums(rows, own_sign, twin_sign):
    def kernel(rows_ref, own_ref, twin_ref, out_ref):
        out_ref[...] = lanes_of(row_sums(rows_ref[...], own_ref[...], twin_ref[...]), 128)

    return pl.pallas_call(kernel, out_shape=jax.ShapeDtypeStruct((rows.shape[0], 128), F32))(
        rows, own_sign, twin_sign
    )


def write_packet(packet_ref, rows, sums, mod, lists, full_width):
    width = rows.shape[1]
    means = [value / full_width for value in sums]
    inv_std = lax.rsqrt(means[1] - means[0] * means[0] + EPS)
    unit_rows = (rows - means[0]) * inv_std
    packet_ref[:, 0:width] = (unit_rows * (1.0 + mod[1:2]) + mod[0:1]).astype(BF16)
    scalars = [inv_std]
    for index in (2, 4):
        scalars += [means[index], (means[index + 1] - means[0] * means[index]) * inv_std]
    high = [value.astype(BF16).astype(F32) for value in scalars]
    low = [value - part for value, part in zip(scalars, high)]
    tail = lanes_of(high + low, 128) + lists.astype(F32)
    packet_ref[:, width:width + 128] = tail.astype(BF16)


def first_packet(rows, sums_own, sums_other, mod, lists, full_width):
    def kernel(rows_ref, own_ref, other_ref, mod_ref, lists_ref, packet_ref):
        sums = own_ref[...] + other_ref[...]
        sums = [sums[:, i:i + 1] for i in range(6)]
        write_packet(packet_ref, rows_ref[...], sums, mod_ref[...], lists_ref[...], full_width)

    height, width = rows.shape
    return pl.pallas_call(kernel, out_shape=jax.ShapeDtypeStruct((height, width + 128), BF16))(
        rows, sums_own, sums_other, mod, lists
    )


def next_packet(rows, branch_own, branch_other, gate, own_sign, twin_sign, mod, lists, step_size):
    def kernel(rows_ref, own_ref, other_ref, gate_ref, own_sign_ref, twin_sign_ref, mod_ref, lists_ref,
               new_ref, packet_ref):
        branch = own_ref[...].astype(F32) + other_ref[...].astype(F32)
        new = rows_ref[...] + step_size * (gate_ref[...] * branch)
        new_ref[...] = new
        sums = row_sums(new, own_sign_ref[...], twin_sign_ref[...])
        write_packet(packet_ref, new, sums, mod_ref[...], lists_ref[...], new.shape[1])

    height, width = rows.shape
    return pl.pallas_call(
        kernel,
        out_shape=[
            jax.ShapeDtypeStruct((height, width), F32),
            jax.ShapeDtypeStruct((height, width + 128), BF16),
        ],
        compiler_params=pltpu.CompilerParams(vmem_limit_bytes=24 * 1024 * 1024),
    )(rows, branch_own, branch_other, gate, own_sign, twin_sign, mod, lists)


def token_scalars(tails, own_half):
    sums = tails[:, 0:5].astype(F32) + tails[:, 5:10].astype(F32)
    if own_half:
        return sums[:, 0:1], sums[:, 1:2], sums[:, 2:3]
    return sums[:, 0:1], sums[:, 3:4], sums[:, 4:5]


def mlp_tangent(pre_hidden, signs, step, consts, tails):
    half, units = pre_hidden[0].shape
    tokens = 2 * half
    lanes = HD if units % HD == 0 else units

    def kernel(own_ref, twin_ref, own_sign_ref, twin_sign_ref, const_ref, own_tail_ref, twin_tail_ref, out_ref):
        own = (0, own_ref, own_tail_ref, own_sign_ref)
        twin = (1, twin_ref, twin_tail_ref, twin_sign_ref)
        for part, pre_ref, tail_ref, sign_ref in (own, twin):
            inv, mean, cross = token_scalars(tail_ref[...], part == 0)
            pre = pre_ref[...]
            tan = inv * (sign_ref[0, :, 0:units].astype(F32) - mean * const_ref[0:1] - cross * (pre - const_ref[1:2]))
            inner = math.sqrt(2.0 / math.pi) * (pre + 0.044715 * (pre * pre * pre))
            bend = jnp.tanh(inner)
            slope = math.sqrt(2.0 / math.pi) * (1.0 + 3.0 * 0.044715 * (pre * pre))
            gelu_slope = 0.5 * (1.0 + bend) + 0.5 * pre * (1.0 - bend * bend) * slope
            product = gelu_slope * tan * sign_ref[0, :, units:2 * units].astype(F32)
            out_ref[pl.ds(part * half, half), :] = sum(product[:, i:i + lanes] for i in range(0, units, lanes))

    def whole(array):
        return pl.BlockSpec(array.shape, lambda i: (0, 0))

    chosen = pl.BlockSpec((1, half, 2 * units), lambda i: (step, 0, 0))
    return pl.pallas_call(
        kernel,
        grid=(1,),
        out_shape=jax.ShapeDtypeStruct((tokens, lanes), F32),
        in_specs=[whole(pre_hidden[0])] * 2 + [chosen] * 2 + [whole(consts)] + [whole(tails[0])] * 2,
        out_specs=pl.BlockSpec((tokens, lanes), lambda i: (0, 0)),
        compiler_params=pltpu.CompilerParams(vmem_limit_bytes=24 * 1024 * 1024),
        cost_estimate=pl.CostEstimate(
            flops=6000 * tokens * units, bytes_accessed=10 * tokens * units, transcendentals=tokens * units
        ),
    )(pre_hidden[0], pre_hidden[1], signs[0], signs[1], consts, tails[0], tails[1])


def normed_head(raw, gain):
    inv = lax.rsqrt(jnp.mean(raw * raw, axis=1, keepdims=True) + EPS)
    return (raw * inv * gain).astype(BF16), inv


def attention(raw_own, raw_twin, bias, q_gain, k_gain, heads):
    queries, tokens = bias.shape
    half = tokens // 2
    scale = 1.0 / math.sqrt(HD)

    def kernel(q_ref, k_ref, v_ref, k_twin_ref, v_twin_ref, bias_ref, qg_ref, kg_ref, out_ref):
        q_n, _ = normed_head(q_ref[...], qg_ref[...])
        k_n = jnp.concatenate(
            [normed_head(k_ref[...], kg_ref[...])[0], normed_head(k_twin_ref[...], kg_ref[...])[0]], axis=0
        )
        v_n = jnp.concatenate([v_ref[...].astype(BF16), v_twin_ref[...].astype(BF16)], axis=0)
        scores = dot_t(q_n, k_n) * scale + bias_ref[...]
        weights = jnp.exp(scores - jnp.max(scores, axis=1, keepdims=True))
        total = jnp.sum(weights, axis=1, keepdims=True)
        out_ref[...] = (dot(weights.astype(BF16), v_n) / total).astype(BF16)

    def columns(part, height):
        return pl.BlockSpec((height, HD), lambda h: (0, part * heads + h))

    return pl.pallas_call(
        kernel,
        grid=(heads,),
        out_shape=jax.ShapeDtypeStruct((queries, heads * HD), BF16),
        in_specs=[
            columns(0, queries),
            columns(1, half),
            columns(2, half),
            columns(1, half),
            columns(2, half),
            pl.BlockSpec((queries, tokens), lambda h: (0, 0)),
            columns(0, 1),
            columns(0, 1),
        ],
        out_specs=columns(0, queries),
        compiler_params=pltpu.CompilerParams(vmem_limit_bytes=20 * 1024 * 1024),
        cost_estimate=pl.CostEstimate(
            flops=30 * heads * queries * tokens * HD,
            bytes_accessed=12 * heads * tokens * HD + 4 * queries * tokens,
            transcendentals=heads * queries * tokens,
        ),
    )(raw_own, raw_own, raw_own, raw_twin, raw_twin, bias, q_gain, k_gain)


def attention_tangent(
    raw, signs, step, consts, tails, bias, q_gain, k_gain, heads
):
    queries, tokens = bias.shape
    scale = 1.0 / math.sqrt(HD)
    half = tokens // 2

    def kernel(q_ref, k_ref, v_ref, q_twin_ref, k_twin_ref, v_twin_ref, qs_ref, ks_ref, vs_ref, back_ref, qs_twin_ref,
               ks_twin_ref, vs_twin_ref, back_twin_ref, qc_ref, kc_ref, vc_ref, tail_ref, tail_twin_ref, bias_ref, qg_ref, kg_ref, out_ref):
        head = pl.program_id(0)
        own = token_scalars(tail_ref[...], True)
        twin = token_scalars(tail_twin_ref[...], False)
        every = [jnp.concatenate(pair, axis=0) for pair in zip(own, twin)]

        def tangent(raw_rows, sign_rows, const_ref, columns):
            inv, mean, cross = columns
            return inv * (
                sign_rows.astype(F32) - mean * const_ref[0:1] - cross * (raw_rows - const_ref[1:2])
            )

        def tangent_head(raw_rows, tan, inv, gain):
            tan_inv = -inv * inv * inv * jnp.mean(raw_rows * tan, axis=1, keepdims=True)
            return ((tan * inv + raw_rows * tan_inv) * gain).astype(BF16)

        k_raw = jnp.concatenate([k_ref[...], k_twin_ref[...]], axis=0)
        k_sign = jnp.concatenate([ks_ref[0], ks_twin_ref[0]], axis=0)
        v_sign = jnp.concatenate([vs_ref[0], vs_twin_ref[0]], axis=0)
        k_n, k_inv = normed_head(k_raw, kg_ref[...])
        dk_n = tangent_head(k_raw, tangent(k_raw, k_sign, kc_ref, every), k_inv, kg_ref[...])
        keys = jnp.concatenate([k_n, dk_n], axis=1)
        v_raw = jnp.concatenate([v_ref[...], v_twin_ref[...]], axis=0)
        v_n = v_raw.astype(BF16)
        values = jnp.concatenate([v_n, tangent(v_raw, v_sign, vc_ref, every).astype(BF16)], axis=1)
        for part in range(2):
            q_raw = (q_twin_ref if part else q_ref)[...]
            q_n, q_inv = normed_head(q_raw, qg_ref[...])
            columns = [column[:queries] for column in (twin if part else own)]
            dq_n = tangent_head(q_raw, tangent(q_raw, (qs_twin_ref if part else qs_ref)[0], qc_ref, columns), q_inv, qg_ref[...])
            scores = dot_t(q_n, k_n) * scale + bias_ref[...]
            weights = jnp.exp(scores - jnp.max(scores, axis=1, keepdims=True))
            inv_total = 1.0 / jnp.sum(weights, axis=1, keepdims=True)
            weighted = weights * (dot_t(jnp.concatenate([dq_n, q_n], axis=1), keys) * scale)
            tan_sum = jnp.sum(weighted, axis=1, keepdims=True) * inv_total
            both = dot(weights.astype(BF16), values) * inv_total
            tan_out = both[:, HD:] + dot(weighted.astype(BF16), v_n) * inv_total - tan_sum * both[:, :HD]
            share = tan_out * (back_twin_ref if part else back_ref)[0].astype(F32)
            span = pl.ds(part * queries, queries)

            @pl.when(head == 0)
            def _():
                out_ref[span, :] = share

            @pl.when(head > 0)
            def _():
                out_ref[span, :] += share

    def columns(part, height):
        return pl.BlockSpec((height, HD), lambda i: (0, part * heads + i))

    def chosen(part, height):
        return pl.BlockSpec((1, height, HD), lambda i: (step, 0, part * heads + i))

    def whole(array):
        return pl.BlockSpec(array.shape, lambda i: (0, 0))

    return pl.pallas_call(
        kernel,
        grid=(heads,),
        out_shape=jax.ShapeDtypeStruct((2 * queries, HD), F32),
        in_specs=[columns(0, queries), columns(1, half), columns(2, half)] * 2
        + [chosen(0, queries), chosen(1, half), chosen(2, half), chosen(3, queries)] * 2
        + [columns(i, consts.shape[0]) for i in range(3)]
        + [whole(tails[0]), whole(tails[1]), whole(bias), columns(0, 1), columns(0, 1)],
        out_specs=pl.BlockSpec((2 * queries, HD), lambda i: (0, 0)),
        compiler_params=pltpu.CompilerParams(vmem_limit_bytes=28 * 1024 * 1024),
        cost_estimate=pl.CostEstimate(
            flops=140 * heads * queries * tokens * HD,
            bytes_accessed=32 * heads * tokens * HD + 4 * queries * tokens,
            transcendentals=2 * heads * queries * tokens,
        ),
    )(
        *[raw[0]] * 3, *[raw[1]] * 3, *[signs[0]] * 4, *[signs[1]] * 4, consts, consts, consts, tails[0], tails[1],
        bias, q_gain, k_gain,
    )


def local(latent, probes, modulation, pattern, w_qkv, w_out, w_up, w_down, q_gain, k_gain):
    ctx_size = lax.axis_size("ctx")
    tp_size = lax.axis_size("tp")
    cycle = cycle_of(ctx_size)
    row_count, local_width = latent.shape
    half = row_count // 2
    full_width = local_width * tp_size
    tokens = row_count * ctx_size
    heads_local = q_gain.shape[0] // HD
    groups = math.gcd(heads_local, ctx_size)
    heads_own = heads_local // groups
    head_width = heads_own * HD
    queries = groups * half
    unit_total = w_up.shape[1]
    units = unit_total // ctx_size
    list_size = pattern.shape[1]
    step_size = 1.0 / STEPS

    ctx_index = lax.axis_index("ctx")
    probe_index = lax.axis_index("probe")
    tp_index = lax.axis_index("tp")
    first = probe_index == 0
    cycle_arr = jnp.array(cycle, jnp.int32)
    place = jnp.array([cycle.index(i) for i in range(ctx_size)], jnp.int32)
    ring_index = place[ctx_index]
    slot_owner = cycle_arr[(ring_index + jnp.arange(-1, ctx_size - 1)) % ctx_size]
    owner_slot = (place - ring_index + 1) % ctx_size
    group = ring_index % groups
    column_offset = (tp_index * local_width).astype(jnp.int32).reshape(1)

    signs_local = (2 * probes[0] - 1).astype(BF16).reshape(2, half, local_width)
    signs_local = jnp.where(first, signs_local, signs_local[::-1]).reshape(row_count, local_width)
    own_sign, twin_sign = signs_local[:half], swap(signs_local[half:], "probe")
    sign_slots = ring_gather(signs_local, cycle, 1)
    lat_half = lax.dynamic_slice_in_dim(latent, probe_index * half, half, 0)
    rows = join_tp(lat_half, 1)
    sign_own = [
        assemble(
            sign_slots, [(k, part * half, half, k * half, "own") for k in range(ctx_size)],
            (ctx_size * half, local_width), 0, column_offset * 0,
        )
        for part in range(2)
    ]
    if tp_size == 2:
        sign_parts = [[own, swap(own, "tp")] for own in sign_own]
        sign_starts = jnp.concatenate([column_offset, local_width - column_offset])
        low = tp_index == 0
        block_signs = [
            jnp.concatenate([jnp.where(low, own, other), jnp.where(low, other, own)], axis=1)
            for own, other in ([part[half:row_count] for part in parts] for parts in sign_parts)
        ]
    else:
        sign_parts = [[lax.all_gather(own, "tp", axis=1, tiled=True)] for own in sign_own]
        sign_starts = column_offset * 0
        block_signs = [parts[0][half:row_count] for parts in sign_parts]
    own_signs, twin_signs = block_signs[0], swap(block_signs[1], "probe")

    qkv_own = lax.dynamic_slice_in_dim(w_qkv, group * head_width, head_width, 2)
    qkv_own = after(jnp.concatenate([qkv_own[:, part] for part in range(3)], axis=1))
    out_own = lax.dynamic_slice_in_dim(w_out, group * head_width, head_width, 0)
    q_gain_own = lax.dynamic_slice_in_dim(q_gain, group * head_width, head_width, 0)[None]
    k_gain_own = lax.dynamic_slice_in_dim(k_gain, group * head_width, head_width, 0)[None]

    stretches = (1.0 + modulation[:, 1]).astype(BF16)
    gates = modulation[:, 2].astype(BF16)
    lists = jnp.pad(pattern.astype(BF16), ((0, 0), (10, 128 - 10 - list_size)))

    half_tokens = ctx_size * half
    mixed = after(jnp.concatenate([qkv_own, out_own.T], axis=1))
    mixed_scales = jnp.stack([stretches] * 3 + [gates])
    unit_scales = jnp.stack([stretches, gates])
    constants = [row for step in range(STEPS) for row in (stretches[step], modulation[step, 0].astype(BF16))]
    constants = jnp.pad(jnp.stack(constants), ((0, 16 - 2 * STEPS), (0, 0)))

    def constant_rows(weight):
        rows = dot(constants, weight)
        return [jnp.pad(rows[2 * step:2 * step + 2], ((0, 6), (0, 0))) for step in range(STEPS)]

    qkv_rows = constant_rows(qkv_own)

    def unit_weights(token):
        late = after(down_own, token)
        up_down.append(after(jnp.concatenate([up_own, late.T], axis=1)))
        return up_down

    def unit_products(part):
        def job(token):
            made = sign_products(sign_parts[part], sign_starts, after(unit_scales, token), up_down[0], units)
            unit_signs.append(made)
            return [made]

        return job

    def head_tangent(step):
        def job(token):
            raw, tails, pre = kept[step]
            share = attention_tangent(
                (after(raw[0], token), raw[1]), head_signs, step, qkv_rows[step], tails, bias, q_gain_own, k_gain_own, heads_own,
            )
            attn_shares.append(share)
            return [share]

        return job

    def unit_tangent(step):
        def job(token):
            raw, tails, pre = kept[step]
            pre_twin = project(after(pre[1], token), up_own, units)
            share = mlp_tangent((pre[0], pre_twin), unit_signs, step, up_rows[step], tails)
            mlp_shares.append(share)
            return [share]

        return job

    def no_job(token):
        return []

    unit_signs, up_down = [], []
    kept, attn_shares, mlp_shares = [], [], []

    bias = None
    for step in range(STEPS):
        mod = modulation[step]
        shift, stretch, gate = mod[0][None], 1.0 + mod[1][None], mod[2][None]

        if step == 0:
            sums = partial_sums(lat_half, own_sign, twin_sign)
            if tp_size == 2:
                sums_other = swap(sums, "tp")
            else:
                sums_other = lax.psum(sums, "tp") - sums
            packet = first_packet(rows, sums, sums_other, mod, lists, full_width)
            packet = after(packet, sign_slots[ctx_size // 2 + 1])
            jobs = [lambda token: sign_own, no_job, no_job, lambda token: sign_parts[0][1:]]
            slots = ring_gather(packet, cycle, 0, jobs)
            at = slots[0].shape[1] - 128 + 10
            listed = jnp.stack([slots[k][0, at:at + list_size] for k in range(groups)]).astype(jnp.int32)
            listed = jnp.any(listed[:, :, None] == slot_owner[None, None, :], axis=1)
            bias = jnp.where(listed, 0.0, NEG_BIG).astype(F32)
            bias = jnp.tile(jnp.repeat(jnp.repeat(bias, half, axis=0), half, axis=1), (1, 2))
        else:
            rows, packet = next_packet(
                rows, branch, branch_other, last_gate, own_signs, twin_signs, mod, lists, step_size
            )
            jobs = [head_tangent(step - 1), unit_products(1), unit_tangent(step - 1)]
            slots = ring_gather(packet, cycle, 0, jobs)
        places = [(k, 0, half, k * half, "all") for k in range(ctx_size)]
        normed, tails = assemble(slots, places, (half_tokens, full_width), 128, column_offset)

        normed_twin, tails_twin = swap(normed, "probe"), swap(tails, "probe")
        if step == 0:
            raw_own = project(normed, qkv_own, head_width)
            raw_twin = project(normed_twin, qkv_own, head_width)
            attended = attention(raw_own, raw_twin, bias, q_gain_own, k_gain_own, heads_own)

            head_signs = [
                sign_products(part, sign_starts, after(mixed_scales, attended), mixed, head_width)
                for part in sign_parts
            ]
            up_part = lax.dynamic_slice_in_dim(w_up, probe_index * (w_up.shape[0] // 2), w_up.shape[0] // 2, 0)
            up_part = up_part.reshape(-1, ctx_size, units).transpose(1, 0, 2)
            down_part = w_down.reshape(ctx_size, 2, units // 2, w_down.shape[1])
            down_part = lax.dynamic_index_in_dim(down_part, probe_index, 1, keepdims=False)
            fused = up_part.shape == down_part.shape
            if fused:
                got = lax.all_to_all(after(after(jnp.stack([up_part, down_part], axis=1)), slots[ctx_size // 2]), "ctx", 0, 0, tiled=True)
                got = after(got, attended, *head_signs)
                got_twin = swap(got, "probe")
                core = probe_index.astype(jnp.int32).reshape(1)
                up_own = place_units(got, got_twin, core, 0)
                down_own = place_units(got, got_twin, core, 1)
            else:
                got = lax.all_to_all(up_part, "ctx", 0, 0, tiled=True)
                pair = jnp.stack([got, swap(got, "probe")], axis=1)
                up_own = jnp.where(first, pair, pair[:, ::-1]).reshape(full_width, units)
                got = lax.all_to_all(down_part, "ctx", 0, 0, tiled=True)
                down_own = join_probe(got.transpose(1, 0, 2).reshape(units // 2, full_width), 0)
            up_rows = constant_rows(up_own)

        parts = []
        if groups < ctx_size:
            pre_own, hidden, far = hidden_units(normed, up_own, down_own, queries)
            parts = [far[k * half:(k + 1) * half] for k in range(ctx_size - groups)]
        else:
            pre_own = dot(normed, up_own)
            hidden = gelu_tanh(pre_own).astype(BF16)
        if step > 0:
            raw_own = dot(normed, qkv_own)
            raw_twin = dot(normed_twin, qkv_own)
            attended = attention(raw_own, raw_twin, bias, q_gain_own, k_gain_own, heads_own)
        near = dot(attended, out_own) + dot(hidden, down_own)
        parts = [near[k * half:(k + 1) * half] for k in range(groups)] + parts

        kept.append(((raw_own, raw_twin), (tails, tails_twin), (pre_own, normed_twin)))
        if step == 0:
            jobs = [no_job, unit_weights, unit_products(0)]
        else:
            jobs = [lambda token: [raw_own], lambda token: [attended], head_tangent(step), unit_tangent(step)]
        branch = ring_reduce(parts, cycle, BF16, jobs).astype(BF16)
        if step == STEPS - 1:
            break
        if tp_size == 2:
            branch_other = swap(branch, "tp")
        else:
            branch_other = sum_tp(branch) - branch.astype(F32)
        last_gate = gate

    estimate = jnp.sum(sum(mlp_shares), axis=1)
    attn_share = jnp.sum(sum(attn_shares), axis=1).reshape(2, queries)
    estimate = estimate + jnp.pad(attn_share, ((0, 0), (0, half_tokens - queries))).reshape(tokens)
    def own_columns(array, index):
        return lax.dynamic_slice_in_dim(array, index * local_width, local_width, 1)

    if tp_size == 2:
        whole = own_columns(branch, tp_index).astype(F32)
        whole = whole + swap(own_columns(branch, 1 - tp_index), "tp").astype(F32)
    else:
        whole = own_columns(sum_tp(branch), tp_index)
    lat_cols = own_columns(rows, tp_index) + step_size * (own_columns(gate, tp_index) * whole)
    latent_out = join_probe(lat_cols, 0)

    by_slot = estimate.reshape(2, ctx_size, half)
    by_slot = jnp.where(first, by_slot, by_slot[::-1]).transpose(1, 0, 2).reshape(ctx_size, row_count)
    by_owner = by_slot[owner_slot][:, None]
    own_estimate = jnp.sum(lax.all_to_all(by_owner, "ctx", 0, 0, tiled=True), axis=0)
    own_estimate = own_estimate + swap(own_estimate, "probe")
    own_estimate = sum_tp(own_estimate)[0]
    density_change = -step_size * own_estimate / (2 * math.sqrt(full_width))
    return (latent_out, density_change)


def solution(mesh):
    return jax.shard_map(
        local,
        mesh=mesh,
        in_specs=(
            P("ctx", "tp"),
            P("probe", "ctx", "tp"),
            P(),
            P("ctx", None),
            P(None, None, "tp"),
            P("tp", None),
            P("ctx", "tp"),
            P("tp", "ctx"),
            P("tp"),
            P("tp"),
        ),
        out_specs=(P("ctx", "tp"), P("ctx")),
        check_vma=False,
    )
```

```python
import math

import jax
import jax.numpy as jnp
from jax import lax
from jax.experimental import pallas as pl
from jax.experimental.pallas import tpu as pltpu
from jax.sharding import PartitionSpec as P

HD = 128
BLK = 128
STEPS = 2
EPS = 1e-06
NEG_BIG = -1e30
F32 = jnp.float32
BF16 = jnp.bfloat16


def after(value, *others):
    return lax.optimization_barrier((value,) + others)[0]


def dot(a, b):
    return jnp.dot(a, b, preferred_element_type=F32)


def dot_t(a, b):
    return lax.dot_general(a, b, (((1,), (1,)), ((), ())), preferred_element_type=F32)


def cycle_of(size):
    return list(range(0, size, 2)) + list(range(size - 1, 0, -2))


def ring_shift(x, cycle, shift):
    size = len(cycle)
    pairs = [(cycle[i], cycle[(i + shift) % size]) for i in range(size)]
    return lax.ppermute(x, "ctx", pairs)


def ring_gather(own, cycle, split_axis, jobs=()):
    size = len(cycle)
    reach = size // 2
    slots = [None] * size
    slots[0] = own
    fore = back = own
    jobs = list(jobs)
    for hop in range(1, reach):
        new_back = ring_shift(back, cycle, 1)
        new_fore = ring_shift(fore, cycle, -1)
        done = jobs.pop(0)(back) if jobs else []
        slots[size - hop], slots[hop] = new_back, new_fore
        back, fore = after(new_back, *done), after(new_fore, *done)
    first = ring_shift(jnp.split(back, 2, axis=split_axis)[0], cycle, 1)
    second = ring_shift(jnp.split(fore, 2, axis=split_axis)[1], cycle, -1)
    done = jobs.pop(0)(back) if jobs else []
    slots[reach] = after(jnp.concatenate([first, second], axis=split_axis), *done)
    return slots[-1:] + slots[:-1]


def ring_reduce(parts, cycle, wire, jobs=()):
    size = len(cycle)
    reach = size // 2
    parts = parts[1:] + parts[:1]
    width = parts[0].shape[1] // 2
    jobs = list(jobs)
    far = parts[reach].astype(wire)
    up = ring_shift(far[:, :width], cycle, 1)
    down = ring_shift(far[:, width:], cycle, -1)
    done = jobs.pop(0)(far) if jobs else []
    up, down = after(up, *done).astype(F32), after(down, *done).astype(F32)
    for hop in range(reach - 1, 0, -1):
        up_part, down_part = parts[hop], parts[size - hop]
        if hop == reach - 1:
            up = jnp.concatenate([up_part[:, :width] + up, up_part[:, width:].astype(F32)], axis=1)
            down = jnp.concatenate([down_part[:, :width].astype(F32), down_part[:, width:] + down], axis=1)
        else:
            up = up_part + up
            down = down_part + down
        up, down = up.astype(wire), down.astype(wire)
        new_up, new_down = ring_shift(up, cycle, 1), ring_shift(down, cycle, -1)
        done = jobs.pop(0)(up) if jobs else []
        up, down = after(new_up, *done).astype(F32), after(new_down, *done).astype(F32)
    return parts[0] + up + down


def swap(x, axis):
    return lax.ppermute(x, axis, [(0, 1), (1, 0)])


def join_tp(own, axis):
    if lax.axis_size("tp") == 2:
        other = swap(own, "tp")
        first = lax.axis_index("tp") == 0
        low = jnp.where(first, own, other)
        high = jnp.where(first, other, own)
        return jnp.concatenate([low, high], axis=axis)
    return lax.all_gather(own, "tp", axis=axis, tiled=True)


def sum_tp(own):
    if lax.axis_size("tp") == 2:
        return own.astype(F32) + swap(own, "tp").astype(F32)
    return jnp.sum(lax.all_gather(own, "tp", axis=0, tiled=False).astype(F32), axis=0)


def join_probe(own, axis):
    other = swap(own, "probe")
    first = lax.axis_index("probe") == 0
    return jnp.concatenate([jnp.where(first, own, other), jnp.where(first, other, own)], axis=axis)


def assemble(pieces, places, shape, tail, offset):
    count = len(places)

    def kernel(offset_ref, *refs):
        ins, out = refs[:len(pieces)], refs[len(pieces)]
        sems = refs[-1]
        base = offset_ref[0]
        copies = []
        for index, (piece, start, height, row, side) in enumerate(places):
            source = ins[piece]
            width = pieces[piece].shape[1]
            if tail and side != "other":
                width -= tail
                copies.append(
                    pltpu.make_async_copy(
                        source.at[pl.ds(start, height), pl.ds(width, tail)],
                        refs[len(pieces) + 1].at[pl.ds(row, height), :],
                        sems.at[count + index],
                    )
                )
            if side == "all":
                target = out.at[pl.ds(row, height), :]
            else:
                column = pl.multiple_of(base if side == "own" else shape[1] - width - base, 128)
                target = out.at[pl.ds(row, height), pl.ds(column, width)]
            main = source.at[pl.ds(start, height), pl.ds(0, width)]
            copies.append(pltpu.make_async_copy(main, target, sems.at[index]))
        for copy in copies:
            copy.start()
        for copy in copies:
            copy.wait()

    size = pieces[0].dtype.itemsize * shape[0] * (shape[1] + tail)
    shapes = [jax.ShapeDtypeStruct(shape, pieces[0].dtype)]
    if tail:
        shapes.append(jax.ShapeDtypeStruct((shape[0], tail), pieces[0].dtype))
    outs = pl.pallas_call(
        kernel,
        out_shape=shapes,
        in_specs=[pl.BlockSpec(memory_space=pltpu.SMEM)] + [pl.BlockSpec(memory_space=pl.ANY)] * len(pieces),
        out_specs=[pl.BlockSpec(memory_space=pltpu.VMEM)] * len(shapes),
        scratch_shapes=[pltpu.SemaphoreType.DMA((2 * count if tail else count,))],
        compiler_params=pltpu.CompilerParams(vmem_limit_bytes=size + 4 * 1024 * 1024),
        cost_estimate=pl.CostEstimate(flops=0, bytes_accessed=2 * size, transcendentals=0),
    )(offset, *pieces)
    return outs if tail else outs[0]


def place_units(own, twin, probe, which):
    size, _, high, wide = own.shape
    shape = (2 * size * high, wide) if which == 0 else (2 * high, size * wide)

    def kernel(probe_ref, own_ref, twin_ref, out, sems):
        me = probe_ref[0]
        copies = []
        for ref, part in ((own_ref, me), (twin_ref, 1 - me)):
            for c in range(size):
                if which == 0:
                    start = pl.multiple_of((2 * c + part) * high, high)
                    target = out.at[pl.ds(start, high), :]
                else:
                    start = pl.multiple_of(part * high, high)
                    target = out.at[pl.ds(start, high), pl.ds(c * wide, wide)]
                copies.append(pltpu.make_async_copy(ref.at[c, which], target, sems.at[len(copies)]))
        for copy in copies:
            copy.start()
        for copy in copies:
            copy.wait()

    size_bytes = own.dtype.itemsize * shape[0] * shape[1]
    return pl.pallas_call(
        kernel,
        out_shape=jax.ShapeDtypeStruct(shape, own.dtype),
        in_specs=[pl.BlockSpec(memory_space=pltpu.SMEM)] + [pl.BlockSpec(memory_space=pl.ANY)] * 2,
        out_specs=pl.BlockSpec(memory_space=pltpu.VMEM),
        scratch_shapes=[pltpu.SemaphoreType.DMA((2 * size,))],
        compiler_params=pltpu.CompilerParams(vmem_limit_bytes=size_bytes + 4 * 1024 * 1024),
        cost_estimate=pl.CostEstimate(flops=0, bytes_accessed=2 * size_bytes, transcendentals=0),
    )(probe, own, twin)


def sign_products(parts, starts, scales, weight, columns):
    tokens = parts[0].shape[0]
    width, total_columns = weight.shape
    blocks, steps, _ = scales.shape
    if columns % 128:
        made = []
        for step in range(steps):
            scaled = [(parts, scales[at, step][None], weight[:, at * columns:(at + 1) * columns]) for at in range(blocks)]
            made.append(jnp.concatenate([dot(signs[0] * scale, own) for signs, scale, own in scaled], axis=1))
        return jnp.stack(made).astype(BF16)

    def kernel(starts_ref, scale_ref, weight_ref, *refs):
        out_ref = refs[-1]
        spans = [
            pl.ds(pl.multiple_of(starts_ref[index], 128), part.shape[1]) for index, part in enumerate(parts)
        ]
        for step in range(steps):
            total = None
            for span, part_ref in zip(spans, refs):
                product = dot(part_ref[...] * scale_ref[0, step:step + 1, span], weight_ref[span, :])
                total = product if total is None else total + product
            out_ref[step] = total.astype(BF16)

    flops = 2 * steps * tokens * width * total_columns
    return pl.pallas_call(
        kernel,
        grid=(blocks,),
        out_shape=jax.ShapeDtypeStruct((steps, tokens, total_columns), BF16),
        in_specs=[
            pl.BlockSpec(memory_space=pltpu.SMEM),
            pl.BlockSpec((1, steps, width), lambda i: (i, 0, 0)),
            pl.BlockSpec((width, columns), lambda i: (0, i)),
        ]
        + [pl.BlockSpec(part.shape, lambda i: (0, 0)) for part in parts],
        out_specs=pl.BlockSpec((steps, tokens, columns), lambda i: (0, 0, i)),
        compiler_params=pltpu.CompilerParams(vmem_limit_bytes=32 * 1024 * 1024),
        cost_estimate=pl.CostEstimate(
            flops=flops + flops // 2,
            bytes_accessed=2 * (tokens * width + width * total_columns + steps * tokens * total_columns),
            transcendentals=0,
        ),
    )(starts, scales, weight, *parts)


def project(rows, weight, columns):
    tokens, width = rows.shape
    total_columns = weight.shape[1]

    def kernel(rows_ref, weight_ref, out_ref):
        out_ref[...] = dot(rows_ref[...], weight_ref[...])

    return pl.pallas_call(
        kernel,
        grid=(total_columns // columns,),
        out_shape=jax.ShapeDtypeStruct((tokens, total_columns), F32),
        in_specs=[
            pl.BlockSpec((tokens, width), lambda i: (0, 0)),
            pl.BlockSpec((width, columns), lambda i: (0, i)),
        ],
        out_specs=pl.BlockSpec((tokens, columns), lambda i: (0, i)),
        compiler_params=pltpu.CompilerParams(vmem_limit_bytes=24 * 1024 * 1024),
        cost_estimate=pl.CostEstimate(
            flops=3 * tokens * width * total_columns,
            bytes_accessed=2 * (tokens * width + width * total_columns) + 4 * tokens * total_columns,
            transcendentals=0,
        ),
    )(rows, weight)


def gelu_tanh(pre):
    inner = math.sqrt(2.0 / math.pi) * (pre + 0.044715 * (pre * pre * pre))
    return 0.5 * pre * (1.0 + jnp.tanh(inner))


def hidden_units(normed, up, down, first_far):
    tokens, width = normed.shape
    units = up.shape[1]

    def kernel(normed_ref, up_ref, down_ref, pre_ref, hidden_ref, far_ref):
        pre = dot(normed_ref[...], up_ref[...])
        pre_ref[...] = pre
        hidden = gelu_tanh(pre).astype(BF16)
        hidden_ref[...] = hidden[:first_far]
        far_ref[...] = dot(hidden[first_far:], down_ref[...]).astype(BF16)

    return pl.pallas_call(
        kernel,
        out_shape=[
            jax.ShapeDtypeStruct((tokens, units), F32),
            jax.ShapeDtypeStruct((first_far, units), BF16),
            jax.ShapeDtypeStruct((tokens - first_far, width), BF16),
        ],
        compiler_params=pltpu.CompilerParams(vmem_limit_bytes=28 * 1024 * 1024),
        cost_estimate=pl.CostEstimate(
            flops=4 * tokens * width * units,
            bytes_accessed=2 * (2 * tokens * width + 2 * width * units),
            transcendentals=tokens * units,
        ),
    )(normed, up, down)


def lanes_of(values, count):
    lane = lax.broadcasted_iota(jnp.int32, (values[0].shape[0], count), 1)
    tile = jnp.zeros(lane.shape, F32)
    for index, value in enumerate(values):
        tile = jnp.where(lane == index, value, tile)
    return tile


def row_sums(rows, own_sign, twin_sign):
    total = [jnp.sum(rows, axis=1, keepdims=True), jnp.sum(rows * rows, axis=1, keepdims=True)]
    for sign in (own_sign.astype(F32), twin_sign.astype(F32)):
        total += [jnp.sum(sign, axis=1, keepdims=True), jnp.sum(rows * sign, axis=1, keepdims=True)]
    return total


def partial_sums(rows, own_sign, twin_sign):
    def kernel(rows_ref, own_ref, twin_ref, out_ref):
        out_ref[...] = lanes_of(row_sums(rows_ref[...], own_ref[...], twin_ref[...]), 128)

    return pl.pallas_call(kernel, out_shape=jax.ShapeDtypeStruct((rows.shape[0], 128), F32))(
        rows, own_sign, twin_sign
    )


def write_packet(packet_ref, rows, sums, mod, lists, full_width):
    width = rows.shape[1]
    means = [value / full_width for value in sums]
    inv_std = lax.rsqrt(means[1] - means[0] * means[0] + EPS)
    unit_rows = (rows - means[0]) * inv_std
    packet_ref[:, 0:width] = (unit_rows * (1.0 + mod[1:2]) + mod[0:1]).astype(BF16)
    scalars = [inv_std]
    for index in (2, 4):
        scalars += [means[index], (means[index + 1] - means[0] * means[index]) * inv_std]
    high = [value.astype(BF16).astype(F32) for value in scalars]
    low = [value - part for value, part in zip(scalars, high)]
    tail = lanes_of(high + low, 128) + lists.astype(F32)
    packet_ref[:, width:width + 128] = tail.astype(BF16)


def first_packet(rows, sums_own, sums_other, mod, lists, full_width):
    def kernel(rows_ref, own_ref, other_ref, mod_ref, lists_ref, packet_ref):
        sums = own_ref[...] + other_ref[...]
        sums = [sums[:, i:i + 1] for i in range(6)]
        write_packet(packet_ref, rows_ref[...], sums, mod_ref[...], lists_ref[...], full_width)

    height, width = rows.shape
    return pl.pallas_call(kernel, out_shape=jax.ShapeDtypeStruct((height, width + 128), BF16))(
        rows, sums_own, sums_other, mod, lists
    )


def next_packet(rows, branch_own, branch_other, gate, own_sign, twin_sign, mod, lists, step_size):
    def kernel(rows_ref, own_ref, other_ref, gate_ref, own_sign_ref, twin_sign_ref, mod_ref, lists_ref,
               new_ref, packet_ref):
        branch = own_ref[...].astype(F32) + other_ref[...].astype(F32)
        new = rows_ref[...] + step_size * (gate_ref[...] * branch)
        new_ref[...] = new
        sums = row_sums(new, own_sign_ref[...], twin_sign_ref[...])
        write_packet(packet_ref, new, sums, mod_ref[...], lists_ref[...], new.shape[1])

    height, width = rows.shape
    return pl.pallas_call(
        kernel,
        out_shape=[
            jax.ShapeDtypeStruct((height, width), F32),
            jax.ShapeDtypeStruct((height, width + 128), BF16),
        ],
        compiler_params=pltpu.CompilerParams(vmem_limit_bytes=24 * 1024 * 1024),
    )(rows, branch_own, branch_other, gate, own_sign, twin_sign, mod, lists)


def token_scalars(tails, own_half):
    sums = tails[:, 0:5].astype(F32) + tails[:, 5:10].astype(F32)
    if own_half:
        return sums[:, 0:1], sums[:, 1:2], sums[:, 2:3]
    return sums[:, 0:1], sums[:, 3:4], sums[:, 4:5]


def mlp_tangent(pre_hidden, signs, step, consts, tails):
    half, units = pre_hidden[0].shape
    tokens = 2 * half
    lanes = HD if units % HD == 0 else units

    def kernel(own_ref, twin_ref, own_sign_ref, twin_sign_ref, const_ref, own_tail_ref, twin_tail_ref, out_ref):
        own = (0, own_ref, own_tail_ref, own_sign_ref)
        twin = (1, twin_ref, twin_tail_ref, twin_sign_ref)
        for part, pre_ref, tail_ref, sign_ref in (own, twin):
            inv, mean, cross = token_scalars(tail_ref[...], part == 0)
            pre = pre_ref[...]
            tan = inv * (sign_ref[0, :, 0:units].astype(F32) - mean * const_ref[0:1] - cross * (pre - const_ref[1:2]))
            inner = math.sqrt(2.0 / math.pi) * (pre + 0.044715 * (pre * pre * pre))
            bend = jnp.tanh(inner)
            slope = math.sqrt(2.0 / math.pi) * (1.0 + 3.0 * 0.044715 * (pre * pre))
            gelu_slope = 0.5 * (1.0 + bend) + 0.5 * pre * (1.0 - bend * bend) * slope
            product = gelu_slope * tan * sign_ref[0, :, units:2 * units].astype(F32)
            out_ref[pl.ds(part * half, half), :] = sum(product[:, i:i + lanes] for i in range(0, units, lanes))

    def whole(array):
        return pl.BlockSpec(array.shape, lambda i: (0, 0))

    chosen = pl.BlockSpec((1, half, 2 * units), lambda i: (step, 0, 0))
    return pl.pallas_call(
        kernel,
        grid=(1,),
        out_shape=jax.ShapeDtypeStruct((tokens, lanes), F32),
        in_specs=[whole(pre_hidden[0])] * 2 + [chosen] * 2 + [whole(consts)] + [whole(tails[0])] * 2,
        out_specs=pl.BlockSpec((tokens, lanes), lambda i: (0, 0)),
        compiler_params=pltpu.CompilerParams(vmem_limit_bytes=24 * 1024 * 1024),
        cost_estimate=pl.CostEstimate(
            flops=6000 * tokens * units, bytes_accessed=10 * tokens * units, transcendentals=tokens * units
        ),
    )(pre_hidden[0], pre_hidden[1], signs[0], signs[1], consts, tails[0], tails[1])


def normed_head(raw, gain):
    inv = lax.rsqrt(jnp.mean(raw * raw, axis=1, keepdims=True) + EPS)
    return (raw * inv * gain).astype(BF16), inv


def attention(raw_own, raw_twin, bias, q_gain, k_gain, heads):
    queries, tokens = bias.shape
    half = tokens // 2
    scale = 1.0 / math.sqrt(HD)

    def kernel(q_ref, k_ref, v_ref, k_twin_ref, v_twin_ref, bias_ref, qg_ref, kg_ref, out_ref):
        q_n, _ = normed_head(q_ref[...], qg_ref[...])
        k_n = jnp.concatenate(
            [normed_head(k_ref[...], kg_ref[...])[0], normed_head(k_twin_ref[...], kg_ref[...])[0]], axis=0
        )
        v_n = jnp.concatenate([v_ref[...].astype(BF16), v_twin_ref[...].astype(BF16)], axis=0)
        scores = dot_t(q_n, k_n) * scale + bias_ref[...]
        weights = jnp.exp(scores - jnp.max(scores, axis=1, keepdims=True))
        total = jnp.sum(weights, axis=1, keepdims=True)
        out_ref[...] = (dot(weights.astype(BF16), v_n) / total).astype(BF16)

    def columns(part, height):
        return pl.BlockSpec((height, HD), lambda h: (0, part * heads + h))

    return pl.pallas_call(
        kernel,
        grid=(heads,),
        out_shape=jax.ShapeDtypeStruct((queries, heads * HD), BF16),
        in_specs=[
            columns(0, queries),
            columns(1, half),
            columns(2, half),
            columns(1, half),
            columns(2, half),
            pl.BlockSpec((queries, tokens), lambda h: (0, 0)),
            columns(0, 1),
            columns(0, 1),
        ],
        out_specs=columns(0, queries),
        compiler_params=pltpu.CompilerParams(vmem_limit_bytes=20 * 1024 * 1024),
        cost_estimate=pl.CostEstimate(
            flops=30 * heads * queries * tokens * HD,
            bytes_accessed=12 * heads * tokens * HD + 4 * queries * tokens,
            transcendentals=heads * queries * tokens,
        ),
    )(raw_own, raw_own, raw_own, raw_twin, raw_twin, bias, q_gain, k_gain)


def attention_tangent(
    raw, signs, step, consts, tails, bias, q_gain, k_gain, heads
):
    queries, tokens = bias.shape
    scale = 1.0 / math.sqrt(HD)
    half = tokens // 2

    def kernel(q_ref, k_ref, v_ref, q_twin_ref, k_twin_ref, v_twin_ref, qs_ref, ks_ref, vs_ref, back_ref, qs_twin_ref,
               ks_twin_ref, vs_twin_ref, back_twin_ref, qc_ref, kc_ref, vc_ref, tail_ref, tail_twin_ref, bias_ref, qg_ref, kg_ref, out_ref):
        head = pl.program_id(0)
        own = token_scalars(tail_ref[...], True)
        twin = token_scalars(tail_twin_ref[...], False)
        every = [jnp.concatenate(pair, axis=0) for pair in zip(own, twin)]

        def tangent(raw_rows, sign_rows, const_ref, columns):
            inv, mean, cross = columns
            return inv * (
                sign_rows.astype(F32) - mean * const_ref[0:1] - cross * (raw_rows - const_ref[1:2])
            )

        def tangent_head(raw_rows, tan, inv, gain):
            tan_inv = -inv * inv * inv * jnp.mean(raw_rows * tan, axis=1, keepdims=True)
            return ((tan * inv + raw_rows * tan_inv) * gain).astype(BF16)

        k_raw = jnp.concatenate([k_ref[...], k_twin_ref[...]], axis=0)
        k_sign = jnp.concatenate([ks_ref[0], ks_twin_ref[0]], axis=0)
        v_sign = jnp.concatenate([vs_ref[0], vs_twin_ref[0]], axis=0)
        k_n, k_inv = normed_head(k_raw, kg_ref[...])
        dk_n = tangent_head(k_raw, tangent(k_raw, k_sign, kc_ref, every), k_inv, kg_ref[...])
        keys = jnp.concatenate([k_n, dk_n], axis=1)
        v_raw = jnp.concatenate([v_ref[...], v_twin_ref[...]], axis=0)
        v_n = v_raw.astype(BF16)
        values = jnp.concatenate([v_n, tangent(v_raw, v_sign, vc_ref, every).astype(BF16)], axis=1)
        for part in range(2):
            q_raw = (q_twin_ref if part else q_ref)[...]
            q_n, q_inv = normed_head(q_raw, qg_ref[...])
            columns = [column[:queries] for column in (twin if part else own)]
            dq_n = tangent_head(q_raw, tangent(q_raw, (qs_twin_ref if part else qs_ref)[0], qc_ref, columns), q_inv, qg_ref[...])
            scores = dot_t(q_n, k_n) * scale + bias_ref[...]
            weights = jnp.exp(scores - jnp.max(scores, axis=1, keepdims=True))
            inv_total = 1.0 / jnp.sum(weights, axis=1, keepdims=True)
            weighted = weights * (dot_t(jnp.concatenate([dq_n, q_n], axis=1), keys) * scale)
            tan_sum = jnp.sum(weighted, axis=1, keepdims=True) * inv_total
            both = dot(weights.astype(BF16), values) * inv_total
            tan_out = both[:, HD:] + dot(weighted.astype(BF16), v_n) * inv_total - tan_sum * both[:, :HD]
            share = tan_out * (back_twin_ref if part else back_ref)[0].astype(F32)
            span = pl.ds(part * queries, queries)

            @pl.when(head == 0)
            def _():
                out_ref[span, :] = share

            @pl.when(head > 0)
            def _():
                out_ref[span, :] += share

    def columns(part, height):
        return pl.BlockSpec((height, HD), lambda i: (0, part * heads + i))

    def chosen(part, height):
        return pl.BlockSpec((1, height, HD), lambda i: (step, 0, part * heads + i))

    def whole(array):
        return pl.BlockSpec(array.shape, lambda i: (0, 0))

    return pl.pallas_call(
        kernel,
        grid=(heads,),
        out_shape=jax.ShapeDtypeStruct((2 * queries, HD), F32),
        in_specs=[columns(0, queries), columns(1, half), columns(2, half)] * 2
        + [chosen(0, queries), chosen(1, half), chosen(2, half), chosen(3, queries)] * 2
        + [columns(i, consts.shape[0]) for i in range(3)]
        + [whole(tails[0]), whole(tails[1]), whole(bias), columns(0, 1), columns(0, 1)],
        out_specs=pl.BlockSpec((2 * queries, HD), lambda i: (0, 0)),
        compiler_params=pltpu.CompilerParams(vmem_limit_bytes=28 * 1024 * 1024),
        cost_estimate=pl.CostEstimate(
            flops=140 * heads * queries * tokens * HD,
            bytes_accessed=32 * heads * tokens * HD + 4 * queries * tokens,
            transcendentals=2 * heads * queries * tokens,
        ),
    )(
        *[raw[0]] * 3, *[raw[1]] * 3, *[signs[0]] * 4, *[signs[1]] * 4, consts, consts, consts, tails[0], tails[1],
        bias, q_gain, k_gain,
    )


def local(latent, probes, modulation, pattern, w_qkv, w_out, w_up, w_down, q_gain, k_gain):
    ctx_size = lax.axis_size("ctx")
    tp_size = lax.axis_size("tp")
    cycle = cycle_of(ctx_size)
    row_count, local_width = latent.shape
    half = row_count // 2
    full_width = local_width * tp_size
    tokens = row_count * ctx_size
    heads_local = q_gain.shape[0] // HD
    groups = math.gcd(heads_local, ctx_size)
    heads_own = heads_local // groups
    head_width = heads_own * HD
    queries = groups * half
    unit_total = w_up.shape[1]
    units = unit_total // ctx_size
    list_size = pattern.shape[1]
    step_size = 1.0 / STEPS

    ctx_index = lax.axis_index("ctx")
    probe_index = lax.axis_index("probe")
    tp_index = lax.axis_index("tp")
    first = probe_index == 0
    cycle_arr = jnp.array(cycle, jnp.int32)
    place = jnp.array([cycle.index(i) for i in range(ctx_size)], jnp.int32)
    ring_index = place[ctx_index]
    slot_owner = cycle_arr[(ring_index + jnp.arange(-1, ctx_size - 1)) % ctx_size]
    owner_slot = (place - ring_index + 1) % ctx_size
    group = ring_index % groups
    column_offset = (tp_index * local_width).astype(jnp.int32).reshape(1)

    signs_local = (2 * probes[0] - 1).astype(BF16).reshape(2, half, local_width)
    signs_local = jnp.where(first, signs_local, signs_local[::-1]).reshape(row_count, local_width)
    own_sign, twin_sign = signs_local[:half], swap(signs_local[half:], "probe")
    sign_slots = ring_gather(signs_local, cycle, 1)
    lat_half = lax.dynamic_slice_in_dim(latent, probe_index * half, half, 0)
    rows = join_tp(lat_half, 1)
    sign_own = [
        assemble(
            sign_slots, [(k, part * half, half, k * half, "own") for k in range(ctx_size)],
            (ctx_size * half, local_width), 0, column_offset * 0,
        )
        for part in range(2)
    ]
    if tp_size == 2:
        sign_parts = [[own, swap(own, "tp")] for own in sign_own]
        sign_starts = jnp.concatenate([column_offset, local_width - column_offset])
        low = tp_index == 0
        block_signs = [
            jnp.concatenate([jnp.where(low, own, other), jnp.where(low, other, own)], axis=1)
            for own, other in ([part[half:row_count] for part in parts] for parts in sign_parts)
        ]
    else:
        sign_parts = [[lax.all_gather(own, "tp", axis=1, tiled=True)] for own in sign_own]
        sign_starts = column_offset * 0
        block_signs = [parts[0][half:row_count] for parts in sign_parts]
    own_signs, twin_signs = block_signs[0], swap(block_signs[1], "probe")

    qkv_own = lax.dynamic_slice_in_dim(w_qkv, group * head_width, head_width, 2)
    qkv_own = after(jnp.concatenate([qkv_own[:, part] for part in range(3)], axis=1))
    out_own = lax.dynamic_slice_in_dim(w_out, group * head_width, head_width, 0)
    q_gain_own = lax.dynamic_slice_in_dim(q_gain, group * head_width, head_width, 0)[None]
    k_gain_own = lax.dynamic_slice_in_dim(k_gain, group * head_width, head_width, 0)[None]

    stretches = (1.0 + modulation[:, 1]).astype(BF16)
    gates = modulation[:, 2].astype(BF16)
    lists = jnp.pad(pattern.astype(BF16), ((0, 0), (10, 128 - 10 - list_size)))

    half_tokens = ctx_size * half
    mixed = after(jnp.concatenate([qkv_own, out_own.T], axis=1))
    mixed_scales = jnp.stack([stretches] * 3 + [gates])
    unit_scales = jnp.stack([stretches, gates])
    constants = [row for step in range(STEPS) for row in (stretches[step], modulation[step, 0].astype(BF16))]
    constants = jnp.pad(jnp.stack(constants), ((0, 16 - 2 * STEPS), (0, 0)))

    def constant_rows(weight):
        rows = dot(constants, weight)
        return [jnp.pad(rows[2 * step:2 * step + 2], ((0, 6), (0, 0))) for step in range(STEPS)]

    qkv_rows = constant_rows(qkv_own)

    def unit_weights(token):
        late = after(down_own, token)
        up_down.append(after(jnp.concatenate([up_own, late.T], axis=1)))
        return up_down

    def unit_products(part):
        def job(token):
            made = sign_products(sign_parts[part], sign_starts, after(unit_scales, token), up_down[0], units)
            unit_signs.append(made)
            return [made]

        return job

    def head_tangent(step):
        def job(token):
            raw, tails, pre = kept[step]
            share = attention_tangent(
                (after(raw[0], token), raw[1]), head_signs, step, qkv_rows[step], tails, bias, q_gain_own, k_gain_own, heads_own,
            )
            attn_shares.append(share)
            return [share]

        return job

    def unit_tangent(step):
        def job(token):
            raw, tails, pre = kept[step]
            pre_twin = project(after(pre[1], token), up_own, units)
            share = mlp_tangent((pre[0], pre_twin), unit_signs, step, up_rows[step], tails)
            mlp_shares.append(share)
            return [share]

        return job

    exchanged = []

    def estimate_exchange(token):
        estimate = jnp.sum(sum(mlp_shares), axis=1)
        attn_share = jnp.sum(sum(attn_shares), axis=1).reshape(2, queries)
        estimate = estimate + jnp.pad(attn_share, ((0, 0), (0, half_tokens - queries))).reshape(tokens)
        by_slot = estimate.reshape(2, ctx_size, half)
        by_slot = jnp.where(first, by_slot, by_slot[::-1]).transpose(1, 0, 2).reshape(ctx_size, row_count)
        by_owner = by_slot[owner_slot][:, None]
        own_estimate = jnp.sum(lax.all_to_all(by_owner, "ctx", 0, 0, tiled=True), axis=0)
        exchanged.append(own_estimate)
        return exchanged

    def no_job(token):
        return []

    unit_signs, up_down = [], []
    kept, attn_shares, mlp_shares = [], [], []

    bias = None
    for step in range(STEPS):
        mod = modulation[step]
        shift, stretch, gate = mod[0][None], 1.0 + mod[1][None], mod[2][None]

        if step == 0:
            sums = partial_sums(lat_half, own_sign, twin_sign)
            if tp_size == 2:
                sums_other = swap(sums, "tp")
            else:
                sums_other = lax.psum(sums, "tp") - sums
            packet = first_packet(rows, sums, sums_other, mod, lists, full_width)
            packet = after(packet, sign_slots[ctx_size // 2 + 1])
            jobs = [lambda token: sign_own, no_job, no_job, lambda token: sign_parts[0][1:]]
            slots = ring_gather(packet, cycle, 0, jobs)
            at = slots[0].shape[1] - 128 + 10
            listed = jnp.stack([slots[k][0, at:at + list_size] for k in range(groups)]).astype(jnp.int32)
            listed = jnp.any(listed[:, :, None] == slot_owner[None, None, :], axis=1)
            bias = jnp.where(listed, 0.0, NEG_BIG).astype(F32)
            bias = jnp.tile(jnp.repeat(jnp.repeat(bias, half, axis=0), half, axis=1), (1, 2))
        else:
            rows, packet = next_packet(
                rows, branch, branch_other, last_gate, own_signs, twin_signs, mod, lists, step_size
            )
            jobs = [head_tangent(step - 1), unit_products(1), unit_tangent(step - 1)]
            slots = ring_gather(packet, cycle, 0, jobs)
        places = [(k, 0, half, k * half, "all") for k in range(ctx_size)]
        normed, tails = assemble(slots, places, (half_tokens, full_width), 128, column_offset)

        normed_twin, tails_twin = swap(normed, "probe"), swap(tails, "probe")
        if step == 0:
            raw_own = project(normed, qkv_own, head_width)
            raw_twin = project(normed_twin, qkv_own, head_width)
            attended = attention(raw_own, raw_twin, bias, q_gain_own, k_gain_own, heads_own)

            head_signs = [
                sign_products(part, sign_starts, after(mixed_scales, attended), mixed, head_width)
                for part in sign_parts
            ]
            up_part = lax.dynamic_slice_in_dim(w_up, probe_index * (w_up.shape[0] // 2), w_up.shape[0] // 2, 0)
            up_part = up_part.reshape(-1, ctx_size, units).transpose(1, 0, 2)
            down_part = w_down.reshape(ctx_size, 2, units // 2, w_down.shape[1])
            down_part = lax.dynamic_index_in_dim(down_part, probe_index, 1, keepdims=False)
            fused = up_part.shape == down_part.shape
            if fused:
                got = lax.all_to_all(after(after(jnp.stack([up_part, down_part], axis=1)), slots[ctx_size // 2]), "ctx", 0, 0, tiled=True)
                got = after(got, attended, *head_signs)
                got_twin = swap(got, "probe")
                core = probe_index.astype(jnp.int32).reshape(1)
                up_own = place_units(got, got_twin, core, 0)
                down_own = place_units(got, got_twin, core, 1)
            else:
                got = lax.all_to_all(up_part, "ctx", 0, 0, tiled=True)
                pair = jnp.stack([got, swap(got, "probe")], axis=1)
                up_own = jnp.where(first, pair, pair[:, ::-1]).reshape(full_width, units)
                got = lax.all_to_all(down_part, "ctx", 0, 0, tiled=True)
                down_own = join_probe(got.transpose(1, 0, 2).reshape(units // 2, full_width), 0)
            up_rows = constant_rows(up_own)

        parts = []
        if groups < ctx_size:
            pre_own, hidden, far = hidden_units(normed, up_own, down_own, queries)
            parts = [far[k * half:(k + 1) * half] for k in range(ctx_size - groups)]
        else:
            pre_own = dot(normed, up_own)
            hidden = gelu_tanh(pre_own).astype(BF16)
        if step > 0:
            raw_own = dot(normed, qkv_own)
            raw_twin = dot(normed_twin, qkv_own)
            attended = attention(raw_own, raw_twin, bias, q_gain_own, k_gain_own, heads_own)
        near = dot(attended, out_own) + dot(hidden, down_own)
        parts = [near[k * half:(k + 1) * half] for k in range(groups)] + parts

        kept.append(((raw_own, raw_twin), (tails, tails_twin), (pre_own, normed_twin)))
        if step == 0:
            jobs = [no_job, unit_weights, unit_products(0)]
        else:
            jobs = [
                lambda token: [raw_own],
                lambda token: [attended] + unit_tangent(step)(attended),
                head_tangent(step),
                estimate_exchange,
            ]
        branch = ring_reduce(parts, cycle, BF16, jobs).astype(BF16)
        if step == STEPS - 1:
            break
        if tp_size == 2:
            branch_other = swap(branch, "tp")
        else:
            branch_other = sum_tp(branch) - branch.astype(F32)
        last_gate = gate

    def own_columns(array, index):
        return lax.dynamic_slice_in_dim(array, index * local_width, local_width, 1)

    if tp_size == 2:
        whole = own_columns(branch, tp_index).astype(F32)
        whole = whole + swap(own_columns(branch, 1 - tp_index), "tp").astype(F32)
    else:
        whole = own_columns(sum_tp(branch), tp_index)
    lat_cols = own_columns(rows, tp_index) + step_size * (own_columns(gate, tp_index) * whole)
    latent_out = join_probe(lat_cols, 0)

    own_estimate = exchanged[0]
    own_estimate = own_estimate + swap(own_estimate, "probe")
    own_estimate = sum_tp(own_estimate)[0]
    density_change = -step_size * own_estimate / (2 * math.sqrt(full_width))
    return (latent_out, density_change)


def solution(mesh):
    return jax.shard_map(
        local,
        mesh=mesh,
        in_specs=(
            P("ctx", "tp"),
            P("probe", "ctx", "tp"),
            P(),
            P("ctx", None),
            P(None, None, "tp"),
            P("tp", None),
            P("ctx", "tp"),
            P("tp", "ctx"),
            P("tp"),
            P("tp"),
        ),
        out_specs=(P("ctx", "tp"), P("ctx")),
        check_vma=False,
    )
```
